128 devices in a mesh: lon: 16 (over y, z_lo, core), lat: 8 (over x, z_hi).
Axes of the slice: x: 4, y: 4, z: 4 (z_hi: 2, z_lo: 2; z = z_hi * 2 + z_lo), core: 2. Of those that a mesh axis runs over, the one named last changes fastest.
Arguments:
- initial_kelvin_map: float32 [1024, 512, 128], P('lon', 'lat'), may hold values from -6 to 6
- thermal_diffusivity_map: float32 [1024, 512, 128], P('lon', 'lat'), may hold values from 0.1 to 1
- interior_power_source: float32 [1024, 512, 128], P('lon', 'lat'), may hold values from -6 to 6
- earlier_east_west_basis: float32 [1024, 32], P('lon'), may hold values from -0.1875 to 0.1875
- earlier_north_south_basis: float32 [512, 32], P('lat'), may hold values from -0.25 to 0.25
- earlier_depthwise_basis: float32 [128, 32], replicated, may hold values from -0.5 to 0.5
Outputs:
- final_kelvin_map: float32 [1024, 512, 128], P('lon', 'lat')
- error: float32 [1024, 512, 128], P('lon', 'lat')
- new_lon: float32 [1024, 32], P('lon')
- new_lat: float32 [512, 32], P('lat')
- new_rad: float32 [128, 32], replicated
- core: float32 [32, 32, 32], replicated
The draws below stay inside these ranges and needn't reach their ends.
All inputs are finite; a program needn't handle non-finite values.
Results may differ from the reference program's by a relative error of at most 0.02.
Values sent between devices are 32-bit elements; how exact they have to be, the bound alone decides.
No kernel may reach another device: no remote copies, remote signals or barrier semaphores. Data moves between devices by JAX's collectives and lax.ppermute only.
A program may use at most 64 MiB of HBM per device.

```python
import math
import jax
import jax.numpy as jnp
from jax import lax

SHELL_LAYERS = 128
R = 32
STEPS = 4
EAST_WEST_SIZE = 1024
NORTH_SOUTH_SIZE = 512


def block_scale(key, dims, split, least, top_value):
    loudness, own = 1.0, jax.random.fold_in(key, 6)
    for dim, parts in split:
        steps = jnp.exp(jax.random.uniform(jax.random.fold_in(own, dim), (parts,), jnp.float32, least / len(split), top_value / len(split)))
        loudness = loudness * jnp.repeat(steps, dims[dim] // parts).reshape([-1 if axis == dim else 1 for axis in range(len(dims))])
    return loudness


def centred(key, shape, scale, limit, split=(), dtype=jnp.bfloat16):
    entries = scale * jax.random.normal(key, shape, jnp.float32)
    if split:
        entries = entries * block_scale(key, shape, split, -0.22, 0.18)
    return jnp.clip(entries, -limit, limit).astype(dtype)


def setup_inputs(seed: int = 0) -> dict:
    key_list = jax.random.split(jax.random.key(seed), 7)
    return {
        "initial_kelvin_map": centred(key_list[0], (EAST_WEST_SIZE, NORTH_SOUTH_SIZE, SHELL_LAYERS), 1.0, 6.0, ((0, 16), (1, 8)), jnp.float32),
        "thermal_diffusivity_map": jnp.clip(jnp.exp(math.log(1.0) - 2.3025851 * jax.random.uniform(key_list[1], (EAST_WEST_SIZE, NORTH_SOUTH_SIZE, SHELL_LAYERS), jnp.float32) ** block_scale(key_list[1], (EAST_WEST_SIZE, NORTH_SOUTH_SIZE, SHELL_LAYERS), ((0, 16), (1, 8)), -0.2, 0.2)), 0.1, 1.0),
        "interior_power_source": centred(key_list[2], (EAST_WEST_SIZE, NORTH_SOUTH_SIZE, SHELL_LAYERS), 1.0, 6.0, ((0, 16), (1, 8)), jnp.float32),
        "earlier_east_west_basis": centred(key_list[3], (EAST_WEST_SIZE, R), EAST_WEST_SIZE ** -0.5, 0.1875, ((0, 16),), jnp.float32),
        "earlier_north_south_basis": centred(key_list[4], (NORTH_SOUTH_SIZE, R), NORTH_SOUTH_SIZE ** -0.5, 0.25, ((0, 8),), jnp.float32),
        "earlier_depthwise_basis": centred(key_list[5], (SHELL_LAYERS, R), SHELL_LAYERS ** -0.5, 0.5, (), jnp.float32),
    }


highest = lax.Precision.HIGHEST
time_step = 0.15

def harmonic(cond_a, cond_b):
    summed = cond_a + cond_b
    return 2.0 * cond_a * cond_b / jnp.where(summed > 0.0, summed, 1.0)

def advance(padded, cond_pad, interior_power_source):
    centre = padded[1:-1, 1:-1]
    kcentre = cond_pad[1:-1, 1:-1]
    change = interior_power_source
    pairs = ((padded[2:, 1:-1], cond_pad[2:, 1:-1]), (padded[:-2, 1:-1], cond_pad[:-2, 1:-1]), (padded[1:-1, 2:], cond_pad[1:-1, 2:]), (padded[1:-1, :-2], cond_pad[1:-1, :-2]))
    for near_t, near_k in pairs:
        change = change + harmonic(kcentre, near_k) * (near_t - centre)
    radial_t = jnp.pad(centre, ((0, 0), (0, 0), (1, 1)))
    radial_k = jnp.pad(kcentre, ((0, 0), (0, 0), (1, 1)))
    change = change + harmonic(kcentre, radial_k[:, :, 2:]) * (radial_t[:, :, 2:] - centre)
    change = change + harmonic(kcentre, radial_k[:, :, :-2]) * (radial_t[:, :, :-2] - centre)
    return centre + time_step * change

def extend(values):
    wrapped = jnp.pad(values, ((1, 1), (0, 0), (0, 0)), mode='wrap')
    return jnp.pad(wrapped, ((0, 0), (1, 1), (0, 0)))

def orthonormal(block, gram):
    factor_l = jnp.linalg.cholesky(gram)
    return lax.linalg.triangular_solve(factor_l, block, left_side=False, lower=True, transpose_a=True)

def refine(modes, factor):
    proj = jnp.dot(modes.T, factor, precision=highest)
    block = jnp.dot(modes, proj, precision=highest)
    gram = jnp.dot(block.T, block, precision=highest)
    return orthonormal(block, gram)

def reference(initial_kelvin_map, thermal_diffusivity_map, interior_power_source, earlier_east_west_basis, earlier_north_south_basis, earlier_depthwise_basis):
    cond_pad = extend(thermal_diffusivity_map)
    final_kelvin_map = initial_kelvin_map
    for step_index in range(STEPS):
        final_kelvin_map = advance(extend(final_kelvin_map), cond_pad, interior_power_source)
    rad_proj = jnp.dot(final_kelvin_map.reshape(EAST_WEST_SIZE * NORTH_SOUTH_SIZE, SHELL_LAYERS), earlier_depthwise_basis, precision=highest).reshape(EAST_WEST_SIZE, NORTH_SOUTH_SIZE, R)
    modes = jnp.einsum('ijb,ja->iab', rad_proj, earlier_north_south_basis, precision=highest).reshape(EAST_WEST_SIZE, R * R)
    new_lon = refine(modes, earlier_east_west_basis)
    modes = jnp.einsum('ijb,ia->jab', rad_proj, new_lon, precision=highest).reshape(NORTH_SOUTH_SIZE, R * R)
    new_lat = refine(modes, earlier_north_south_basis)
    lon_proj = jnp.dot(new_lon.T, final_kelvin_map.reshape(EAST_WEST_SIZE, NORTH_SOUTH_SIZE * SHELL_LAYERS), precision=highest).reshape(R, NORTH_SOUTH_SIZE, SHELL_LAYERS)
    modes = jnp.einsum('ajr,jb->rab', lon_proj, new_lat, precision=highest).reshape(SHELL_LAYERS, R * R)
    new_rad = refine(modes, earlier_depthwise_basis)
    core = jnp.einsum('rab,rc->abc', modes.reshape(SHELL_LAYERS, R, R), new_rad, precision=highest)
    first = jnp.einsum('abc,rc->abr', core, new_rad, precision=highest)
    second = jnp.einsum('abr,jb->ajr', first, new_lat, precision=highest)
    recon = jnp.dot(new_lon, second.reshape(R, NORTH_SOUTH_SIZE * SHELL_LAYERS), precision=highest).reshape(EAST_WEST_SIZE, NORTH_SOUTH_SIZE, SHELL_LAYERS)
    return (final_kelvin_map, final_kelvin_map - recon, new_lon, new_lat, new_rad, core)
```

```python
import functools

import jax
import jax.numpy as jnp
from jax import lax
from jax.experimental import pallas as pl
from jax.experimental.pallas import tpu as pltpu
from jax.sharding import PartitionSpec as P

SHELL_LAYERS = 128
R = 32
STEPS = 4
time_step = 0.15
highest = lax.Precision.HIGHEST
W = STEPS


def dot(a, b, ca, cb):
    return lax.dot_general(
        a, b, (((ca,), (cb,)), ((), ())), precision=highest, preferred_element_type=jnp.float32
    )


def face(p, q):
    summed = p + q
    return (2.0 * time_step) * p * q / jnp.where(summed > 0.0, summed, 1.0)


def conduct_kernel(n, m, t_ref, k_ref, s_ref, below_ref, above_ref, south_ref, north_ref,
                   ssouth_ref, snorth_ref, out_ref, t, k, s, hx, hy, hz):
    rows = m + 2 * W
    layers = t_ref.shape[2]
    tile = (2 * W, layers)
    first = lax.broadcasted_iota(jnp.int32, tile, 0) < W
    half = (n + 2 * W) // 2

    def inner(i, c):
        t[i + W, 0:m, :] = t_ref[i]
        k[i + W, 0:m, :] = k_ref[i]
        s[i + W, 0:m, :] = s_ref[i] * time_step
        return c

    lax.fori_loop(0, n, inner, 0, unroll=2)
    for i in range(W):
        t[i, 0:m, :] = below_ref[i]
        k[i, 0:m, :] = below_ref[W + i]
        t[n + W + i, 0:m, :] = above_ref[i]
        k[n + W + i, 0:m, :] = above_ref[W + i]
        s[i, 0:m, :] = below_ref[2 * W + i] * time_step
        s[n + W + i, 0:m, :] = above_ref[2 * W + i] * time_step

    def edge(i, c):
        south, north = south_ref[i], north_ref[i]
        t[i, m:rows, :] = jnp.where(first, north, south)
        k[i, m:rows, :] = pltpu.roll(jnp.where(first, south, north), W, 0)
        return c

    lax.fori_loop(0, n + 2 * W, edge, 0, unroll=2)

    def edge_s(i, c):
        south, north = ssouth_ref[i] * time_step, snorth_ref[i] * time_step
        s[i, m:rows, :] = jnp.where(first, north, pltpu.roll(south, W, 0))
        s[i + half, m:rows, :] = jnp.where(first, pltpu.roll(north, W, 0), south)
        return c

    lax.fori_loop(0, half, edge_s, 0, unroll=2)

    inside = lax.broadcasted_iota(jnp.int32, (rows, layers), 1) < layers - 1

    def faces(i, c):
        kc = k[i]
        hx[i] = face(kc, k[jnp.minimum(i + 1, n + 2 * W - 1)])
        hy[i] = face(kc, pltpu.roll(kc, rows - 1, 0))
        hz[i] = jnp.where(inside, face(kc, pltpu.roll(kc, layers - 1, 1)), 0.0)
        return c

    lax.fori_loop(0, n + 2 * W, faces, 0)

    for step in range(STEPS):
        last = step == STEPS - 1

        def body(p, carry):
            tc, fprev = carry
            tn = t[p + 1]
            fx = hx[p] * (tn - tc)
            fy = hy[p] * (pltpu.roll(tc, rows - 1, 0) - tc)
            fz = hz[p] * (pltpu.roll(tc, layers - 1, 1) - tc)
            new = tc + (
                (s[p] + (fx - fprev))
                + ((fy - pltpu.roll(fy, 1, 0)) + (fz - pltpu.roll(fz, 1, 1)))
            )
            if last:
                out_ref[p - W] = new[0:m]
            else:
                t[p] = new
            return tn, fx

        tc = t[step + 1]
        lax.fori_loop(
            step + 1, n + 2 * W - 1 - step, body, (tc, hx[step] * (tc - t[step])), unroll=2
        )


def conduct(t, k, s):
    n, m, layers = t.shape
    lon, lat = lax.axis_size("lon"), lax.axis_size("lat")
    up = [(i, (i + 1) % lon) for i in range(lon)]
    down = [(j, i) for i, j in up]
    below = lax.ppermute(jnp.concatenate([t[n - W:], k[n - W:], s[n - W:]], 0), "lon", up)
    above = lax.ppermute(jnp.concatenate([t[:W], k[:W], s[:W]], 0), "lon", down)

    def ext(x, q, lo):
        rows = slice(0, W) if lo else slice(m - W, m)
        return jnp.concatenate(
            [below[q * W:q * W + W, rows], x[:, rows], above[q * W:q * W + W, rows]], 0
        )

    north_to = [(i, i + 1) for i in range(lat - 1)]
    south_to = [(j, i) for i, j in north_to]
    half = (n + 2 * W) // 2
    low_s, high_s = ext(s, 2, True), ext(s, 2, False)
    south = lax.ppermute(jnp.concatenate([ext(k, 1, False), ext(t, 0, False)], 1), "lat", north_to)
    north = lax.ppermute(jnp.concatenate([ext(t, 0, True), ext(k, 1, True)], 1), "lat", south_to)
    ssouth = lax.ppermute(jnp.concatenate([high_s[:half], high_s[half:]], 1), "lat", north_to)
    snorth = lax.ppermute(jnp.concatenate([low_s[:half], low_s[half:]], 1), "lat", south_to)
    big = pltpu.VMEM((n + 2 * W, m + 2 * W, layers), jnp.float32)
    return pl.pallas_call(
        functools.partial(conduct_kernel, n, m),
        out_shape=jax.ShapeDtypeStruct(t.shape, jnp.float32),
        in_specs=[pl.BlockSpec(memory_space=pltpu.VMEM)] * 9,
        out_specs=pl.BlockSpec(memory_space=pltpu.VMEM),
        scratch_shapes=[big] * 6,
        compiler_params=pltpu.CompilerParams(vmem_limit_bytes=48 * 2**20),
        name="conduct",
    )(t, k, s, below, above, south, north, ssouth, snorth)


def inverse_factor(gram):
    n = gram.shape[0]
    row = lax.broadcasted_iota(jnp.int32, (n, n), 0)
    col = lax.broadcasted_iota(jnp.int32, (n, n), 1)
    a = gram
    inv = jnp.where(row == col, 1.0, 0.0).astype(jnp.float32)
    scale = jnp.zeros((n, 1), jnp.float32)
    r1 = lax.broadcasted_iota(jnp.int32, (n, 1), 0)
    for j in range(n):
        column = a[:, j:j + 1]
        pivot = a[j:j + 1, j:j + 1]
        factor = jnp.where(r1 > j, column / pivot, 0.0)
        scale = jnp.where(r1 == j, lax.rsqrt(pivot), scale)
        a = a - factor * a[j:j + 1, :]
        inv = inv - factor * inv[j:j + 1, :]
    return inv * scale


def inverse_kernel(g_ref, o_ref):
    o_ref[...] = inverse_factor(g_ref[...])


def inverse(gram):
    return pl.pallas_call(
        inverse_kernel, out_shape=jax.ShapeDtypeStruct(gram.shape, jnp.float32), name="inverse"
    )(gram)


def scatter_sum(parts, axis):
    return jnp.sum(lax.all_to_all(parts, axis, 0, 0, tiled=True), axis=0)


def gather(part, axis):
    count = lax.axis_size(axis)
    return lax.all_to_all(
        jnp.broadcast_to(part[None], (count,) + part.shape), axis, 0, 0, tiled=True
    )


def total(part, axis):
    return jnp.sum(gather(part, axis), axis=0)


def local(t0, k, s, u, v, w):
    n, m, layers = t0.shape
    lon, lat = lax.axis_size("lon"), lax.axis_size("lat")
    t = conduct(t0, k, s)
    rad = dot(t.reshape(n * m, layers), w, 1, 0).reshape(n, m, R)
    parts = jnp.einsum("ijb,ja->iab", rad, v, precision=highest)
    parts = parts.reshape(n, lat, R // lat * R).transpose(1, 0, 2)
    y1 = scatter_sum(parts, "lat")
    proj = total(dot(u, y1, 0, 0), "lon")
    b1 = total(dot(proj, y1, 1, 1), "lat")
    g1 = dot(b1, b1, 1, 1)
    bs = R // lon
    parts = jnp.einsum("ijb,ci->bjc", rad, b1, precision=highest).reshape(lon, bs * m * R // 128, 128)
    parts = jnp.concatenate(
        [parts, jnp.broadcast_to(g1.reshape(1, R * R // 128, 128), (lon, R * R // 128, 128))], 1
    )
    got = scatter_sum(parts, "lon")
    y2 = got[: bs * m * R // 128].reshape(bs * m, R)
    inv1 = inverse(got[bs * m * R // 128:].reshape(R, R))
    new_lon = dot(b1, inv1, 0, 1)
    y2 = dot(y2, inv1, 1, 1).reshape(bs, m, R)
    proj = total(jnp.einsum("jc,bja->cba", v, y2, precision=highest).reshape(R, bs * R), "lat")
    b2 = jnp.einsum("bja,cba->cj", y2, proj.reshape(R, bs, R), precision=highest)
    b2 = total(b2.reshape(R * m // 128, 128), "lon").reshape(R, m)
    g2 = dot(b2, b2, 1, 1)
    lonp = jnp.einsum("ia,ijr->ajr", new_lon, t, precision=highest)
    parts = jnp.einsum("ajr,bj->arb", lonp, b2, precision=highest)
    parts = parts.reshape(lon, (R // lon) * layers * R // 128, 128)
    got = scatter_sum(parts, "lon")
    size = got.shape[0]
    got = total(jnp.concatenate([got, g2.reshape(R * R // 128, 128)], 0), "lat")
    y3 = gather(got[:size], "lon").reshape(R * layers, R)
    inv2 = inverse(got[size:].reshape(R, R))
    new_lat = dot(b2, inv2, 0, 1)
    y3 = dot(y3, inv2, 1, 1).reshape(R, layers, R)
    proj = jnp.einsum("arb,rc->cab", y3, w, precision=highest)
    b3 = jnp.einsum("arb,cab->rc", y3, proj, precision=highest)
    inv3 = inverse(dot(b3, b3, 0, 0))
    new_rad = dot(b3, inv3, 1, 1)
    core = jnp.einsum("arb,rc->abc", y3, new_rad, precision=highest)
    first = jnp.einsum("abc,rc->abr", core, new_rad, precision=highest)
    second = jnp.einsum("abr,jb->ajr", first, new_lat, precision=highest)
    recon = dot(new_lon, second.reshape(R, m * layers), 1, 0).reshape(n, m, layers)
    return (t, t - recon, new_lon, new_lat, new_rad, core)


def solution(mesh):
    grid = P("lon", "lat", None)
    return jax.shard_map(
        local,
        mesh=mesh,
        in_specs=(grid, grid, grid, P("lon", None), P("lat", None), P()),
        out_specs=(grid, grid, P("lon", None), P("lat", None), P(), P()),
        check_vma=False,
    )
```

```python
import functools

import jax
import jax.numpy as jnp
from jax import lax
from jax.experimental import pallas as pl
from jax.experimental.pallas import tpu as pltpu
from jax.sharding import PartitionSpec as P

SHELL_LAYERS = 128
R = 32
STEPS = 4
time_step = 0.15
highest = lax.Precision.HIGHEST
W = STEPS


def dot(a, b, ca, cb):
    return lax.dot_general(
        a, b, (((ca,), (cb,)), ((), ())), precision=highest, preferred_element_type=jnp.float32
    )


def halves(x):
    high = x.astype(jnp.bfloat16)
    return high, (x - high.astype(jnp.float32)).astype(jnp.bfloat16)


def dot3(a, b, ca=1, cb=0):
    ah, al = halves(a) if not isinstance(a, tuple) else a
    bh, bl = halves(b) if not isinstance(b, tuple) else b

    def one(x, y):
        return lax.dot_general(
            x, y, (((ca,), (cb,)), ((), ())), preferred_element_type=jnp.float32
        )

    return one(ah, bh) + (one(ah, bl) + one(al, bh))


PAD = 4
TILE = PAD + W
SENT = 3 * W - 1


def pack_lat_kernel(t0, k0, s0, t1, k1, s1, low_ref, high_ref):
    n = t0.shape[0]
    for q in range(W):
        low_ref[q] = t0[:, q, :]
        low_ref[W + q] = k0[:, q, :]
        high_ref[q] = t1[:, TILE - W + q, :]
        high_ref[W + q] = k1[:, TILE - W + q, :]
    for q in range(W - 1):
        low_ref[2 * W + q] = s0[:, q, :]
        high_ref[2 * W + q] = s1[:, TILE - W + 1 + q, :]


def pack_lon_kernel(t0, k0, s0, t1, k1, s1, low_ref, high_ref):
    low_ref[0:W] = t0[...]
    low_ref[W:2 * W] = k0[...]
    low_ref[2 * W:] = s0[0:W - 1]
    high_ref[0:W] = t1[...]
    high_ref[W:2 * W] = k1[...]
    high_ref[2 * W:] = s1[1:W]


def pack(kernel, block, dim, t, k, s, slab, name):
    count = t.shape[dim] // block[dim]

    def spec(place):
        return pl.BlockSpec(block, lambda g: tuple(place if d == dim else 0 for d in range(3)))

    shape = jax.ShapeDtypeStruct((SENT,) + slab, jnp.float32)
    return pl.pallas_call(
        kernel,
        grid=(1,),
        out_shape=(shape, shape),
        in_specs=[spec(0)] * 3 + [spec(count - 1)] * 3,
        out_specs=[pl.BlockSpec(shape.shape, lambda g: (0, 0, 0))] * 2,
        name=name,
    )(t, k, s, t, k, s)


def face(p, q):
    summed = p + q
    return (2.0 * time_step) * p * q / jnp.where(summed > 0.0, summed, 1.0)


def conduct_kernel(n, m, lat, t_ref, k_ref, s_ref, below_ref, above_ref, south_ref, north_ref,
                   csouth_ref, cnorth_ref, v_ref, w_ref, out_ref, parts_ref,
                   ta, tb, k, s, hx, hy, hz, z, sems):
    layers = t_ref.shape[2]
    planes = n + 2 * W
    end = TILE + m
    copies = [
        pltpu.make_async_copy(src, dst.at[W:n + W, TILE:end, :], sems.at[i])
        for i, (src, dst) in enumerate(((t_ref, ta), (k_ref, k), (s_ref, s)))
    ]
    for copy in copies:
        copy.start()
    for q in range(SENT):
        arr, at = ((ta, q), (k, q - W), (s, q - 2 * W))[q // W]
        late = q // W == 2
        low_row = PAD + at + (1 if late else 0)
        arr[W:n + W, low_row, :] = south_ref[q]
        arr[W:n + W, end + at, :] = north_ref[q]
        low_plane = at + (1 if late else 0)
        high_plane = n + W + at
        arr[low_plane, TILE:end, :] = below_ref[q]
        arr[high_plane, TILE:end, :] = above_ref[q]
        arr[low_plane, PAD:TILE, :] = csouth_ref[q, 0:W]
        arr[high_plane, PAD:TILE, :] = csouth_ref[q, W:2 * W]
        arr[low_plane, end:end + W, :] = cnorth_ref[q, 0:W]
        arr[high_plane, end:end + W, :] = cnorth_ref[q, W:2 * W]
    for copy in copies:
        copy.wait()

    rows = slice(PAD, end + W)
    count = m + 2 * W
    inside = lax.broadcasted_iota(jnp.int32, (count, layers), 1) < layers - 1

    def faces(i, kc):
        kn = k[i + 1, rows, :]
        hx[i, rows, :] = face(kc, kn)
        hy[i, rows, :] = face(kc, k[i, PAD + 1:PAD + 1 + count, :])
        hz[i, rows, :] = jnp.where(inside, face(kc, pltpu.roll(kc, layers - 1, 1)), 0.0)
        return kn

    lax.fori_loop(0, planes - 1, faces, k[0, rows, :], unroll=4)

    for step in range(STEPS):
        last = step == STEPS - 1
        src, dst = (ta, tb) if step % 2 == 0 else (tb, ta)
        lo, num = (TILE, m) if last else (PAD, count)

        def body(p, carry):
            tc, before = carry
            tn = src[p + 1, lo:lo + num, :]
            fx = hx[p, lo:lo + num, :] * (tn - tc)
            fn = hy[p, lo:lo + num, :] * (src[p, lo + 1:lo + 1 + num, :] - tc)
            fs = hy[p, lo - 1:lo - 1 + num, :] * (src[p, lo - 1:lo - 1 + num, :] - tc)
            up = hz[p, lo:lo + num, :]
            fu = up * (pltpu.roll(tc, layers - 1, 1) - tc)
            fd = pltpu.roll(up, 1, 1) * (pltpu.roll(tc, 1, 1) - tc)
            new = tc + ((s[p, lo:lo + num, :] * time_step + (fx - before)) + ((fn + fs) + (fu + fd)))
            if last:
                out_ref[p - W] = new
            else:
                dst[p, lo:lo + num, :] = new
            return tn, fx

        tc = src[step + 1, lo:lo + num, :]
        start = hx[step, lo:lo + num, :] * (tc - src[step, lo:lo + num, :])
        lax.fori_loop(step + 1, planes - 1 - step, body, (tc, start), unroll=8)

    share = R // lat
    vh, vl = halves(v_ref[...])
    lhs = jnp.concatenate([vh, vh, vl], axis=1)

    def project(i, c):
        pair = jnp.concatenate([out_ref[2 * i], out_ref[2 * i + 1]], axis=1)
        high, low = halves(pair)
        got = lax.dot_general(
            lhs, jnp.concatenate([high, low, high], axis=0), (((1,), (0,)), ((), ())),
            preferred_element_type=jnp.float32,
        )
        for e in range(2):
            for a in range(share):
                z[a, pl.ds(2 * i + e, lat, stride=n), :] = got[
                    a * lat:(a + 1) * lat, e * layers:(e + 1) * layers
                ]
        return c

    lax.fori_loop(0, n // 2, project, 0, unroll=4)
    lane = lax.broadcasted_iota(jnp.int32, w_ref.shape, 1) // R
    total = None
    for a in range(share):
        part = dot3(z[a], jnp.where(lane == a, w_ref[...], 0.0))
        total = part if total is None else total + part
    parts_ref[...] = total


def conduct(t, k, s, v, w):
    n, m, layers = t.shape
    lon, lat = lax.axis_size("lon"), lax.axis_size("lat")
    north_to = [(i, i + 1) for i in range(lat - 1)]
    south_to = [(j, i) for i, j in north_to]
    up = [(i, (i + 1) % lon) for i in range(lon)]
    down = [(j, i) for i, j in up]
    low, high = pack(pack_lat_kernel, (n, TILE, layers), 1, t, k, s, (n, layers), "pack_lat")
    south = lax.ppermute(high, "lat", north_to)
    north = lax.ppermute(low, "lat", south_to)
    low, high = pack(pack_lon_kernel, (W, m, layers), 0, t, k, s, (m, layers), "pack_lon")
    below = lax.ppermute(high, "lon", up)
    above = lax.ppermute(low, "lon", down)
    csouth = lax.ppermute(jnp.concatenate([below[:, m - W:], above[:, m - W:]], 1), "lat", north_to)
    cnorth = lax.ppermute(jnp.concatenate([below[:, :W], above[:, :W]], 1), "lat", south_to)
    share = R // lat
    vt = v.reshape(m, lat, share).transpose(2, 1, 0).reshape(R, m)
    big = pltpu.VMEM((n + 2 * W, m + 2 * TILE, layers), jnp.float32)
    vmem = pl.BlockSpec(memory_space=pltpu.VMEM)
    return pl.pallas_call(
        functools.partial(conduct_kernel, n, m, lat),
        out_shape=(
            jax.ShapeDtypeStruct(t.shape, jnp.float32),
            jax.ShapeDtypeStruct((lat * n, share * R), jnp.float32),
        ),
        in_specs=[pl.BlockSpec(memory_space=pl.ANY)] * 3 + [vmem] * 8,
        out_specs=[vmem] * 2,
        scratch_shapes=[big] * 7
        + [pltpu.VMEM((share, lat * n, layers), jnp.float32), pltpu.SemaphoreType.DMA((3,))],
        compiler_params=pltpu.CompilerParams(vmem_limit_bytes=52 * 2**20),
        name="conduct",
    )(t, k, s, below, above, south, north, csouth, cnorth, vt, jnp.tile(w, (1, share)))


def inverse_factor(gram):
    n = gram.shape[0]
    row = lax.broadcasted_iota(jnp.int32, (n, n), 0)
    col = lax.broadcasted_iota(jnp.int32, (n, n), 1)
    a = gram
    inv = jnp.where(row == col, 1.0, 0.0).astype(jnp.float32)
    scale = jnp.zeros((n, 1), jnp.float32)
    r1 = lax.broadcasted_iota(jnp.int32, (n, 1), 0)
    for j in range(n):
        column = a[:, j:j + 1]
        pivot = a[j:j + 1, j:j + 1]
        factor = jnp.where(r1 > j, column / pivot, 0.0)
        scale = jnp.where(r1 == j, lax.rsqrt(pivot), scale)
        a = a - factor * a[j:j + 1, :]
        inv = inv - factor * inv[j:j + 1, :]
    return inv * scale


def call(kernel, name, outs, args, scratch=(), cost=None, aliases=None):
    vmem = pl.BlockSpec(memory_space=pltpu.VMEM)
    return pl.pallas_call(
        kernel,
        out_shape=tuple(jax.ShapeDtypeStruct(o, jnp.float32) for o in outs),
        in_specs=[vmem] * len(args),
        out_specs=(vmem,) * len(outs),
        scratch_shapes=list(scratch),
        compiler_params=pltpu.CompilerParams(vmem_limit_bytes=40 * 2**20),
        cost_estimate=cost,
        name=name,
    )(*args)


def cost(us):
    return pl.CostEstimate(flops=0, bytes_accessed=int(us * 3e6), transcendentals=0)


def add_up(ref):
    total = ref[0]
    for i in range(1, ref.shape[0]):
        total = total + ref[i]
    return total


def send_all(ref, x):
    for i in range(ref.shape[0]):
        ref[i] = x


def widen(x, n):
    k = x.shape[0] // n
    return jnp.concatenate([x[i * k:(i + 1) * k] for i in range(n)], axis=1)


def narrow(x, n):
    c = x.shape[1] // n
    return jnp.concatenate([x[:, i * c:(i + 1) * c] for i in range(n)], axis=0)


def eye(n):
    row = lax.broadcasted_iota(jnp.int32, (n, n), 0)
    return jnp.where(row == lax.broadcasted_iota(jnp.int32, (n, n), 1), 1.0, 0.0).astype(jnp.float32)


def flip(x):
    return dot(eye(x.shape[1]), x, 1, 1)


def diagonal(x, n):
    k = x.shape[0]
    wide = jnp.concatenate([x] * n, axis=1)
    wide = jnp.concatenate([wide] * n, axis=0)
    row = lax.broadcasted_iota(jnp.int32, wide.shape, 0) // k
    col = lax.broadcasted_iota(jnp.int32, wide.shape, 1) // k
    return jnp.where(row == col, wide, 0.0)


def stack_left(x):
    high, low = halves(x)
    return jnp.concatenate([high, high, low], axis=1)


def stack_right(x):
    high, low = halves(x)
    return jnp.concatenate([high, low, high], axis=0)


def product(left, right):
    return lax.dot_general(
        left, right, (((1,), (0,)), ((), ())), preferred_element_type=jnp.float32
    )


def lon_project_kernel(got, ut, y1, out):
    y = add_up(got)
    y1[...] = y
    send_all(out, dot(ut[...], y, 1, 0))


def lon_block_kernel(got, y1, out):
    send_all(out, widen(dot(add_up(got), y1[...], 1, 1), 2))


def radial_kernel(m, t, wt, out):
    n = t.shape[0] // m
    half = m // 2
    share = out.shape[0]
    peers = R // share
    w = halves(wt[...])

    def body(j, c):
        x = jnp.concatenate(
            [t[pl.ds(j + h * half, n, stride=m), :] for h in range(2)], axis=0
        )
        got = dot3(w, x, 1, 1)
        for b in range(share):
            out[b, pl.ds(j, peers, stride=half), :] = got[b * peers:(b + 1) * peers]
        return c

    lax.fori_loop(0, half, body, 0, unroll=4)


def lat_modes_kernel(got, rt, out, b1):
    block = narrow(add_up(got), 2)
    b1[...] = block
    gram = widen(dot(block, block, 1, 1), 4)
    wide = jnp.concatenate([block, block], axis=1)
    wide = jnp.concatenate([wide] * 4, axis=0)
    row = lax.broadcasted_iota(jnp.int32, wide.shape, 0) // R
    half = lax.broadcasted_iota(jnp.int32, wide.shape, 1) // block.shape[1]
    total = None
    for b in range(rt.shape[0]):
        part = dot3(rt[b], jnp.where(row == 2 * b + half, wide, 0.0), 1, 1)
        total = part if total is None else total + part
    rows = total.shape[0] // out.shape[0]
    for i in range(out.shape[0]):
        out[i, 0:rows] = total[i * rows:(i + 1) * rows]
        out[i, rows:] = gram


def lat_project_kernel(got, b1, vt, out, y2, lon, lont):
    total = add_up(got)
    gram = narrow(total[total.shape[0] - R // 4:], 4)
    inv = inverse_factor(gram)
    block = b1[...]
    lont[...] = dot(inv, block, 1, 0)
    lon[...] = dot(flip(block), inv, 1, 1)
    y = dot(total[:total.shape[0] - R // 4], diagonal(inv, 4), 1, 1)
    y2[...] = y
    half = vt.shape[1] // 2
    lane = lax.broadcasted_iota(jnp.int32, (R, y.shape[1]), 1) // R % 2
    send_all(
        out,
        jnp.where(
            lane == 0, dot(vt[:, 0:half], y, 1, 0), dot(vt[:, half:], y, 1, 0)
        ),
    )


def lon_sums_kernel(m, t, lont, out):
    n = t.shape[0] // m
    layers = t.shape[1]
    left = stack_left(lont[...])

    def body(j, c):
        x = jnp.concatenate([t[pl.ds(2 * j + e, n, stride=m), :] for e in range(2)], axis=1)
        got = product(left, stack_right(x))
        for e in range(2):
            out[pl.ds(2 * j + e, R, stride=m), :] = got[:, e * layers:(e + 1) * layers]
        return c

    lax.fori_loop(0, m // 2, body, 0, unroll=4)


def lat_block_kernel(got, y2, out):
    q = add_up(got)
    y = y2[...]
    lane = lax.broadcasted_iota(jnp.int32, q.shape, 1) // R % 2
    width = q.shape[1]
    both = q + jnp.where(lane == 0, pltpu.roll(q, width - R, 1), pltpu.roll(q, R, 1))
    side = lax.broadcasted_iota(jnp.int32, y.shape, 1) // R % 2
    rows = jnp.concatenate([jnp.where(side == 0, y, 0.0), jnp.where(side == 1, y, 0.0)], axis=0)
    send_all(out, widen(dot(both, rows, 1, 1), 2))


def radial_modes_kernel(got, lp, out, b2, g2):
    block = narrow(add_up(got), 2)
    b2[...] = block
    g2[...] = widen(dot(block, block, 1, 1), 4)
    left = stack_left(block)
    m = block.shape[1]
    layers = lp.shape[1]

    def body(a, c):
        x = jnp.concatenate(
            [lp[pl.ds(pl.multiple_of((2 * a + e) * m, m), m), :] for e in range(2)], axis=1
        )
        y = product(left, stack_right(x))
        for e in range(2):
            out[a, e * R:(e + 1) * R, :] = y[:, e * layers:(e + 1) * layers]
        return c

    lax.fori_loop(0, R // 2, body, 0, unroll=4)


def radial_sum_kernel(got, g2, out):
    total = add_up(got)
    for i in range(out.shape[0]):
        out[i, 0:total.shape[0]] = total
        out[i, total.shape[0]:] = g2[...]


def radial_spread_kernel(got, out, g2):
    total = add_up(got)
    rows = out.shape[1]
    send_all(out, total[:rows])
    g2[...] = total[rows:]


def lat_factor_kernel(g2, b2, inv, lat):
    inverse = inverse_factor(narrow(g2[...], 4))
    inv[...] = inverse
    lat[...] = dot(flip(b2[...]), inverse, 1, 1)


def last_kernel(m, y3_ref, inv2, lat, lon, wt, t, err, rad, core_ref, y3, first, second):
    layers = y3.shape[1]
    n = t.shape[0] // m
    mix = halves(diagonal(inv2[...], layers // R))
    for i in range(y3.shape[0] // layers):
        y3[i * layers:(i + 1) * layers] = dot3(mix, y3_ref[i * layers:(i + 1) * layers])
    y = halves(y3[...])
    proj = dot3(wt[...], y, 1, 1)
    block = dot3(proj, y)
    inv = inverse_factor(dot(block, block, 1, 1))
    radt = dot(inv, block, 1, 0)
    rad[...] = flip(radt)
    radh = halves(radt)
    core = dot3(y, radh, 1, 1)
    core_ref[...] = core
    first[...] = dot3(core, radh)
    left = stack_left(lat[...])

    def widen_lat(a, c):
        x = jnp.concatenate(
            [first[pl.ds(pl.multiple_of((2 * a + e) * R, R), R), :] for e in range(2)], axis=1
        )
        got = product(left, stack_right(x))
        for e in range(2):
            at = pl.multiple_of((2 * a + e) * m, m)
            second[pl.ds(at, m), :] = got[:, e * layers:(e + 1) * layers]
        return c

    lax.fori_loop(0, R // 2, widen_lat, 0, unroll=4)
    lonl = stack_left(lon[...])

    def widen_lon(j, c):
        x = jnp.concatenate(
            [second[pl.ds(2 * j + e, R, stride=m), :] for e in range(2)], axis=1
        )
        got = product(lonl, stack_right(x))
        for e in range(2):
            at = pl.ds(2 * j + e, n, stride=m)
            err[at, :] = t[at, :] - got[:, e * layers:(e + 1) * layers]
        return c

    lax.fori_loop(0, m // 2, widen_lon, 0, unroll=4)


def exchange(parts, axis):
    return lax.all_to_all(parts, axis, 0, 0, tiled=True)


def local(t0, k, s, u, v, w):
    n, m, layers = t0.shape
    lon, lat = lax.axis_size("lon"), lax.axis_size("lat")
    t, parts = conduct(t0, k, s, v, w)
    flat = t.reshape(n * m, layers)
    share = R // lon
    wt = w.T
    vt = v.T
    wide = R // lat * R
    got = exchange(parts.reshape(lat, n, wide), "lat")
    (rt,) = call(
        functools.partial(radial_kernel, m), "radial",
        [(share, lon * m // 2, 2 * n)],
        [flat, wt.reshape(lon, share, layers).transpose(1, 0, 2).reshape(R, layers)],
        cost=cost(4),
    )
    y1, parts = call(
        lon_project_kernel, "lon_project", [(n, wide), (lon, R, wide)], [got, u.T]
    )
    (parts,) = call(
        lon_block_kernel, "lon_block", [(lat, R // 2, 2 * n)], [exchange(parts, "lon"), y1]
    )
    parts, b1 = call(
        lat_modes_kernel, "lat_modes", [(lon, m // 2 + R // 4, 2 * share * R), (R, n)],
        [exchange(parts, "lat"), rt],
    )
    parts, y2, new_lon, lont = call(
        lat_project_kernel, "lat_project",
        [(lat, R, 2 * share * R), (m // 2, 2 * share * R), (n, R), (R, n)],
        [exchange(parts, "lon"), b1, vt],
    )
    got = exchange(parts, "lat")
    (lp,) = call(
        functools.partial(lon_sums_kernel, m), "lon_sums", [(R * m, layers)], [flat, lont],
        cost=cost(4),
    )
    (parts,) = call(lat_block_kernel, "lat_block", [(lon, R // 2, 2 * m)], [got, y2])
    parts, b2, g2 = call(
        radial_modes_kernel, "radial_modes",
        [(lon, share * R, layers), (R, m), (R // 4, 4 * R)],
        [exchange(parts, "lon"), lp],
    )
    (parts,) = call(
        radial_sum_kernel, "radial_sum", [(lat, share * R + R // 4, layers)],
        [exchange(parts, "lon"), g2],
    )
    parts, g2 = call(
        radial_spread_kernel, "radial_spread", [(lon, share * R, layers), (R // 4, 4 * R)],
        [exchange(parts, "lat")],
    )
    got = exchange(parts, "lon")
    inv2, new_lat = call(
        lat_factor_kernel, "lat_factor", [(R, R), (m, R)], [g2, b2], cost=cost(4)
    )
    err, new_rad, core = call(
        functools.partial(last_kernel, m), "last",
        [(n * m, layers), (layers, R), (R * R, R)],
        [got.reshape(R * R, layers), inv2, new_lat, new_lon, wt, flat],
        scratch=[
            pltpu.VMEM((R * R, layers), jnp.float32),
            pltpu.VMEM((R * R, layers), jnp.float32),
            pltpu.VMEM((R * m, layers), jnp.float32),
        ],
    )
    return (t, err.reshape(n, m, layers), new_lon, new_lat, new_rad, core.reshape(R, R, R))


def solution(mesh):
    grid = P("lon", "lat", None)
    return jax.shard_map(
        local,
        mesh=mesh,
        in_specs=(grid, grid, grid, P("lon", None), P("lat", None), P()),
        out_specs=(grid, grid, P("lon", None), P("lat", None), P(), P()),
        check_vma=False,
    )
```

```python
import functools

import jax
import jax.numpy as jnp
from jax import lax
from jax.experimental import pallas as pl
from jax.experimental.pallas import tpu as pltpu
from jax.sharding import PartitionSpec as P

SHELL_LAYERS = 128
R = 32
STEPS = 4
time_step = 0.15
highest = lax.Precision.HIGHEST
W = STEPS


def dot(a, b, ca, cb):
    return lax.dot_general(
        a, b, (((ca,), (cb,)), ((), ())), precision=highest, preferred_element_type=jnp.float32
    )


def halves(x):
    high = x.astype(jnp.bfloat16)
    return high, (x - high.astype(jnp.float32)).astype(jnp.bfloat16)


def dot3(a, b, ca=1, cb=0):
    ah, al = halves(a) if not isinstance(a, tuple) else a
    bh, bl = halves(b) if not isinstance(b, tuple) else b

    def one(x, y):
        return lax.dot_general(
            x, y, (((ca,), (cb,)), ((), ())), preferred_element_type=jnp.float32
        )

    return one(ah, bh) + (one(ah, bl) + one(al, bh))


PAD = 4
TILE = PAD + W
SENT = 3 * W - 1


def pack_lat_kernel(t0, k0, s0, t1, k1, s1, low_ref, high_ref):
    n = t0.shape[0]
    for q in range(W):
        low_ref[q] = t0[:, q, :]
        low_ref[W + q] = k0[:, q, :]
        high_ref[q] = t1[:, TILE - W + q, :]
        high_ref[W + q] = k1[:, TILE - W + q, :]
    for q in range(W - 1):
        low_ref[2 * W + q] = s0[:, q, :]
        high_ref[2 * W + q] = s1[:, TILE - W + 1 + q, :]


def pack_lon_kernel(t0, k0, s0, t1, k1, s1, low_ref, high_ref):
    low_ref[0:W] = t0[...]
    low_ref[W:2 * W] = k0[...]
    low_ref[2 * W:] = s0[0:W - 1]
    high_ref[0:W] = t1[...]
    high_ref[W:2 * W] = k1[...]
    high_ref[2 * W:] = s1[1:W]


def pack(kernel, block, dim, t, k, s, slab, name):
    count = t.shape[dim] // block[dim]

    def spec(place):
        return pl.BlockSpec(block, lambda g: tuple(place if d == dim else 0 for d in range(3)))

    shape = jax.ShapeDtypeStruct((SENT,) + slab, jnp.float32)
    return pl.pallas_call(
        kernel,
        grid=(1,),
        out_shape=(shape, shape),
        in_specs=[spec(0)] * 3 + [spec(count - 1)] * 3,
        out_specs=[pl.BlockSpec(shape.shape, lambda g: (0, 0, 0))] * 2,
        name=name,
    )(t, k, s, t, k, s)


def face(p, q):
    summed = p + q
    return (2.0 * time_step) * p * q / jnp.where(summed > 0.0, summed, 1.0)


def conduct_kernel(n, m, lat, t_ref, k_ref, s_ref, below_ref, above_ref, south_ref, north_ref,
                   csouth_ref, cnorth_ref, v_ref, w_ref, out_ref, parts_ref,
                   ta, tb, k, s, hx, hy, hz, hd, full, z, sems):
    layers = t_ref.shape[2]
    planes = n + 2 * W
    end = TILE + m
    copies = [
        pltpu.make_async_copy(src, dst.at[W:n + W, TILE:end, :], sems.at[i])
        for i, (src, dst) in enumerate(((k_ref, k), (t_ref, ta), (s_ref, s)))
    ]
    for copy in copies:
        copy.start()
    for q in range(SENT):
        arr, at = ((ta, q), (k, q - W), (s, q - 2 * W))[q // W]
        late = q // W == 2
        low_row = PAD + at + (1 if late else 0)
        arr[W:n + W, low_row, :] = south_ref[q]
        arr[W:n + W, end + at, :] = north_ref[q]
        low_plane = at + (1 if late else 0)
        high_plane = n + W + at
        arr[low_plane, TILE:end, :] = below_ref[q]
        arr[high_plane, TILE:end, :] = above_ref[q]
        arr[low_plane, PAD:TILE, :] = csouth_ref[q, 0:W]
        arr[high_plane, PAD:TILE, :] = csouth_ref[q, W:2 * W]
        arr[low_plane, end:end + W, :] = cnorth_ref[q, 0:W]
        arr[high_plane, end:end + W, :] = cnorth_ref[q, W:2 * W]
    copies[0].wait()

    rows = slice(PAD, end + W)
    count = m + 2 * W
    inside = lax.broadcasted_iota(jnp.int32, (count, layers), 1) < layers - 1

    def faces(i, kc):
        kn = k[i + 1, rows, :]
        hx[i, rows, :] = face(kc, kn)
        hy[i, rows, :] = face(kc, k[i, PAD + 1:PAD + 1 + count, :])
        up = jnp.where(inside, face(kc, pltpu.roll(kc, layers - 1, 1)), 0.0)
        hz[i, rows, :] = up
        hd[i, rows, :] = pltpu.roll(up, 1, 1)
        return kn

    lax.fori_loop(0, planes - 1, faces, k[0, rows, :], unroll=4)

    copies[1].wait()
    copies[2].wait()
    for step in range(STEPS):
        last = step == STEPS - 1
        src, dst = (ta, tb) if step % 2 == 0 else (tb, ta)
        lo, num = (TILE, m) if last else (PAD, count)

        def body(p, carry):
            tc, before = carry
            tn = src[p + 1, lo:lo + num, :]
            fx = hx[p, lo:lo + num, :] * (tn - tc)
            fn = hy[p, lo:lo + num, :] * (src[p, lo + 1:lo + 1 + num, :] - tc)
            fs = hy[p, lo - 1:lo - 1 + num, :] * (src[p, lo - 1:lo - 1 + num, :] - tc)
            fu = hz[p, lo:lo + num, :] * (pltpu.roll(tc, layers - 1, 1) - tc)
            fd = hd[p, lo:lo + num, :] * (pltpu.roll(tc, 1, 1) - tc)
            gain = s[p, lo:lo + num, :]
            if step == 0:
                gain = gain * time_step
                s[p, lo:lo + num, :] = gain
            new = tc + ((gain + (fx - before)) + ((fn + fs) + (fu + fd)))
            if last:
                full[p - W] = new
            else:
                dst[p, lo:lo + num, :] = new
            return tn, fx

        tc = src[step + 1, lo:lo + num, :]
        start = hx[step, lo:lo + num, :] * (tc - src[step, lo:lo + num, :])
        lax.fori_loop(step + 1, planes - 1 - step, body, (tc, start), unroll=16)

    written = pltpu.make_async_copy(full, out_ref, sems.at[0])
    written.start()
    share = R // lat
    row = lax.broadcasted_iota(jnp.int32, (R, R), 0)
    col = lax.broadcasted_iota(jnp.int32, (R, R), 1)
    order = jnp.where(row % lat * share + row // lat == col, 1.0, 0.0).astype(jnp.float32)
    vh, vl = halves(dot(order, v_ref[...], 1, 0))
    lhs = jnp.concatenate([vh, vh, vl], axis=1)

    def project(i, c):
        pair = jnp.concatenate([full[2 * i], full[2 * i + 1]], axis=1)
        high, low = halves(pair)
        got = lax.dot_general(
            lhs, jnp.concatenate([high, low, high], axis=0), (((1,), (0,)), ((), ())),
            preferred_element_type=jnp.float32,
        )
        for e in range(2):
            for a in range(share):
                z[a, pl.ds(2 * i + e, lat, stride=n), :] = got[
                    a * lat:(a + 1) * lat, e * layers:(e + 1) * layers
                ]
        return c

    lax.fori_loop(0, n // 2, project, 0, unroll=4)
    tiled = jnp.concatenate([w_ref[...]] * share, axis=0)
    block = lax.broadcasted_iota(jnp.int32, tiled.shape, 0) // R
    total = None
    for a in range(share):
        part = dot3(z[a], jnp.where(block == a, tiled, 0.0), 1, 1)
        total = part if total is None else total + part
    parts_ref[...] = total
    written.wait()


def conduct(t, k, s, v, w):
    n, m, layers = t.shape
    lon, lat = lax.axis_size("lon"), lax.axis_size("lat")
    north_to = [(i, i + 1) for i in range(lat - 1)]
    south_to = [(j, i) for i, j in north_to]
    up = [(i, (i + 1) % lon) for i in range(lon)]
    down = [(j, i) for i, j in up]
    low, high = pack(pack_lat_kernel, (n, TILE, layers), 1, t, k, s, (n, layers), "pack_lat")
    south = lax.ppermute(high, "lat", north_to)
    north = lax.ppermute(low, "lat", south_to)
    low, high = pack(pack_lon_kernel, (W, m, layers), 0, t, k, s, (m, layers), "pack_lon")
    below = lax.ppermute(high, "lon", up)
    above = lax.ppermute(low, "lon", down)
    csouth = lax.ppermute(jnp.concatenate([below[:, m - W:], above[:, m - W:]], 1), "lat", north_to)
    cnorth = lax.ppermute(jnp.concatenate([below[:, :W], above[:, :W]], 1), "lat", south_to)
    share = R // lat
    big = pltpu.VMEM((n + 2 * W, m + 2 * TILE, layers), jnp.float32)
    vmem = pl.BlockSpec(memory_space=pltpu.VMEM)
    return pl.pallas_call(
        functools.partial(conduct_kernel, n, m, lat),
        out_shape=(
            jax.ShapeDtypeStruct(t.shape, jnp.float32),
            jax.ShapeDtypeStruct((lat * n, share * R), jnp.float32),
        ),
        in_specs=[pl.BlockSpec(memory_space=pl.ANY)] * 3 + [vmem] * 8,
        out_specs=[pl.BlockSpec(memory_space=pl.ANY), vmem],
        scratch_shapes=[big] * 8
        + [pltpu.VMEM(t.shape, jnp.float32), pltpu.VMEM((share, lat * n, layers), jnp.float32), pltpu.SemaphoreType.DMA((3,))],
        compiler_params=pltpu.CompilerParams(vmem_limit_bytes=56 * 2**20),
        name="conduct",
    )(t, k, s, below, above, south, north, csouth, cnorth, v.T, w.T)


def inverse_factor(gram):
    n = gram.shape[0]
    row = lax.broadcasted_iota(jnp.int32, (n, n), 0)
    col = lax.broadcasted_iota(jnp.int32, (n, n), 1)
    a = gram
    inv = jnp.where(row == col, 1.0, 0.0).astype(jnp.float32)
    scale = jnp.zeros((n, 1), jnp.float32)
    r1 = lax.broadcasted_iota(jnp.int32, (n, 1), 0)
    for j in range(n):
        column = a[:, j:j + 1]
        pivot = a[j:j + 1, j:j + 1]
        factor = jnp.where(r1 > j, column / pivot, 0.0)
        scale = jnp.where(r1 == j, lax.rsqrt(pivot), scale)
        a = a - factor * a[j:j + 1, :]
        inv = inv - factor * inv[j:j + 1, :]
    return inv * scale


def call(kernel, name, outs, args, scratch=(), cost=None, aliases=None):
    vmem = pl.BlockSpec(memory_space=pltpu.VMEM)
    return pl.pallas_call(
        kernel,
        out_shape=tuple(jax.ShapeDtypeStruct(o, jnp.float32) for o in outs),
        in_specs=[vmem] * len(args),
        out_specs=(vmem,) * len(outs),
        scratch_shapes=list(scratch),
        compiler_params=pltpu.CompilerParams(vmem_limit_bytes=40 * 2**20),
        cost_estimate=cost,
        name=name,
    )(*args)


def cost(us):
    return pl.CostEstimate(flops=0, bytes_accessed=int(us * 3e6), transcendentals=0)


def add_up(ref):
    total = ref[0]
    for i in range(1, ref.shape[0]):
        total = total + ref[i]
    return total


def send_all(ref, x):
    for i in range(ref.shape[0]):
        ref[i] = x


def widen(x, n):
    k = x.shape[0] // n
    return jnp.concatenate([x[i * k:(i + 1) * k] for i in range(n)], axis=1)


def narrow(x, n):
    c = x.shape[1] // n
    return jnp.concatenate([x[:, i * c:(i + 1) * c] for i in range(n)], axis=0)


def eye(n):
    row = lax.broadcasted_iota(jnp.int32, (n, n), 0)
    return jnp.where(row == lax.broadcasted_iota(jnp.int32, (n, n), 1), 1.0, 0.0).astype(jnp.float32)


def flip(x):
    return dot(eye(x.shape[1]), x, 1, 1)


def diagonal(x, n):
    k = x.shape[0]
    wide = jnp.concatenate([x] * n, axis=1)
    wide = jnp.concatenate([wide] * n, axis=0)
    row = lax.broadcasted_iota(jnp.int32, wide.shape, 0) // k
    col = lax.broadcasted_iota(jnp.int32, wide.shape, 1) // k
    return jnp.where(row == col, wide, 0.0)


def stack_left(x):
    high, low = halves(x)
    return jnp.concatenate([high, high, low], axis=1)


def stack_right(x):
    high, low = halves(x)
    return jnp.concatenate([high, low, high], axis=0)


def product(left, right):
    return lax.dot_general(
        left, right, (((1,), (0,)), ((), ())), preferred_element_type=jnp.float32
    )


def lon_project_kernel(got, ut, y1, out):
    y = add_up(got)
    y1[...] = y
    send_all(out, dot(ut[...], y, 1, 0))


def lon_block_kernel(got, y1, out):
    send_all(out, widen(dot(add_up(got), y1[...], 1, 1), 2))


def radial_kernel(m, t, wt, out):
    n = t.shape[0] // m
    half = m // 2
    share = out.shape[0]
    peers = R // share
    w = halves(wt[...])

    def body(j, c):
        x = jnp.concatenate(
            [t[pl.ds(j + h * half, n, stride=m), :] for h in range(2)], axis=0
        )
        got = dot3(w, x, 1, 1)
        for b in range(share):
            out[b, pl.ds(j, peers, stride=half), :] = got[b * peers:(b + 1) * peers]
        return c

    lax.fori_loop(0, half, body, 0, unroll=4)


def lat_modes_kernel(got, rt, out, b1):
    block = narrow(add_up(got), 2)
    b1[...] = block
    gram = widen(dot(block, block, 1, 1), 4)
    wide = jnp.concatenate([block, block], axis=1)
    wide = jnp.concatenate([wide] * 4, axis=0)
    row = lax.broadcasted_iota(jnp.int32, wide.shape, 0) // R
    half = lax.broadcasted_iota(jnp.int32, wide.shape, 1) // block.shape[1]
    total = None
    for b in range(rt.shape[0]):
        part = dot3(rt[b], jnp.where(row == 2 * b + half, wide, 0.0), 1, 1)
        total = part if total is None else total + part
    rows = total.shape[0] // out.shape[0]
    for i in range(out.shape[0]):
        out[i, 0:rows] = total[i * rows:(i + 1) * rows]
        out[i, rows:] = gram


def lat_project_kernel(got, b1, vt, out, y2, lon, lont):
    total = add_up(got)
    gram = narrow(total[total.shape[0] - R // 4:], 4)
    inv = inverse_factor(gram)
    block = b1[...]
    lont[...] = dot(inv, block, 1, 0)
    lon[...] = dot(flip(block), inv, 1, 1)
    y = dot(total[:total.shape[0] - R // 4], diagonal(inv, 4), 1, 1)
    y2[...] = y
    half = vt.shape[1] // 2
    lane = lax.broadcasted_iota(jnp.int32, (R, y.shape[1]), 1) // R % 2
    send_all(
        out,
        jnp.where(
            lane == 0, dot(vt[:, 0:half], y, 1, 0), dot(vt[:, half:], y, 1, 0)
        ),
    )


def lon_sums_kernel(m, t, lont, out):
    n = t.shape[0] // m
    layers = t.shape[1]
    left = stack_left(lont[...])

    def body(j, c):
        x = jnp.concatenate([t[pl.ds(2 * j + e, n, stride=m), :] for e in range(2)], axis=1)
        got = product(left, stack_right(x))
        for e in range(2):
            out[pl.ds(2 * j + e, R, stride=m), :] = got[:, e * layers:(e + 1) * layers]
        return c

    lax.fori_loop(0, m // 2, body, 0, unroll=4)


def lat_block_kernel(got, y2, out):
    q = add_up(got)
    y = y2[...]
    lane = lax.broadcasted_iota(jnp.int32, q.shape, 1) // R % 2
    width = q.shape[1]
    both = q + jnp.where(lane == 0, pltpu.roll(q, width - R, 1), pltpu.roll(q, R, 1))
    side = lax.broadcasted_iota(jnp.int32, y.shape, 1) // R % 2
    rows = jnp.concatenate([jnp.where(side == 0, y, 0.0), jnp.where(side == 1, y, 0.0)], axis=0)
    send_all(out, widen(dot(both, rows, 1, 1), 2))


def radial_modes_kernel(got, lp, out, b2, g2):
    block = narrow(add_up(got), 2)
    b2[...] = block
    g2[...] = widen(dot(block, block, 1, 1), 4)
    left = stack_left(block)
    m = block.shape[1]
    layers = lp.shape[1]

    def body(a, c):
        x = jnp.concatenate(
            [lp[pl.ds(pl.multiple_of((2 * a + e) * m, m), m), :] for e in range(2)], axis=1
        )
        y = product(left, stack_right(x))
        for e in range(2):
            out[a, e * R:(e + 1) * R, :] = y[:, e * layers:(e + 1) * layers]
        return c

    lax.fori_loop(0, R // 2, body, 0, unroll=4)


def radial_sum_kernel(got, g2, out):
    total = add_up(got)
    for i in range(out.shape[0]):
        out[i, 0:total.shape[0]] = total
        out[i, total.shape[0]:] = g2[...]


def radial_spread_kernel(got, out, g2):
    total = add_up(got)
    rows = out.shape[1]
    send_all(out, total[:rows])
    g2[...] = total[rows:]


def lat_factor_kernel(g2, b2, inv, lat):
    inverse = inverse_factor(narrow(g2[...], 4))
    inv[...] = inverse
    lat[...] = dot(flip(b2[...]), inverse, 1, 1)


def last_kernel(m, y3_ref, inv2, lat, lon, wt, t, err, rad, core_ref, y3, first, second):
    layers = y3.shape[1]
    n = t.shape[0] // m
    mix = halves(diagonal(inv2[...], layers // R))
    for i in range(y3.shape[0] // layers):
        y3[i * layers:(i + 1) * layers] = dot3(mix, y3_ref[i * layers:(i + 1) * layers])
    y = halves(y3[...])
    proj = dot3(wt[...], y, 1, 1)
    block = dot3(proj, y)
    inv = inverse_factor(dot(block, block, 1, 1))
    radt = dot(inv, block, 1, 0)
    rad[...] = radt
    radh = halves(radt)
    core = dot3(y, radh, 1, 1)
    core_ref[...] = core
    first[...] = dot3(core, radh)
    left = stack_left(lat[...])

    def widen_lat(a, c):
        x = jnp.concatenate(
            [first[pl.ds(pl.multiple_of((2 * a + e) * R, R), R), :] for e in range(2)], axis=1
        )
        got = product(left, stack_right(x))
        for e in range(2):
            at = pl.multiple_of((2 * a + e) * m, m)
            second[pl.ds(at, m), :] = got[:, e * layers:(e + 1) * layers]
        return c

    lax.fori_loop(0, R // 2, widen_lat, 0, unroll=4)
    lonl = stack_left(lon[...])

    def widen_lon(j, c):
        x = jnp.concatenate(
            [second[pl.ds(2 * j + e, R, stride=m), :] for e in range(2)], axis=1
        )
        got = product(lonl, stack_right(x))
        for e in range(2):
            at = pl.ds(2 * j + e, n, stride=m)
            err[at, :] = t[at, :] - got[:, e * layers:(e + 1) * layers]
        return c

    lax.fori_loop(0, m // 2, widen_lon, 0, unroll=4)


def exchange(parts, axis):
    return lax.all_to_all(parts, axis, 0, 0, tiled=True)


def local(t0, k, s, u, v, w):
    n, m, layers = t0.shape
    lon, lat = lax.axis_size("lon"), lax.axis_size("lat")
    t, parts = conduct(t0, k, s, v, w)
    flat = t.reshape(n * m, layers)
    share = R // lon
    wt = w.T
    vt = v.T
    wide = R // lat * R
    got = exchange(parts.reshape(lat, n, wide), "lat")
    (rt,) = call(
        functools.partial(radial_kernel, m), "radial",
        [(share, lon * m // 2, 2 * n)],
        [flat, wt.reshape(lon, share, layers).transpose(1, 0, 2).reshape(R, layers)],
        cost=cost(4),
    )
    y1, parts = call(
        lon_project_kernel, "lon_project", [(n, wide), (lon, R, wide)], [got, u.T]
    )
    (parts,) = call(
        lon_block_kernel, "lon_block", [(lat, R // 2, 2 * n)], [exchange(parts, "lon"), y1]
    )
    parts, b1 = call(
        lat_modes_kernel, "lat_modes", [(lon, m // 2 + R // 4, 2 * share * R), (R, n)],
        [exchange(parts, "lat"), rt],
    )
    parts, y2, new_lon, lont = call(
        lat_project_kernel, "lat_project",
        [(lat, R, 2 * share * R), (m // 2, 2 * share * R), (n, R), (R, n)],
        [exchange(parts, "lon"), b1, vt],
    )
    got = exchange(parts, "lat")
    (lp,) = call(
        functools.partial(lon_sums_kernel, m), "lon_sums", [(R * m, layers)], [flat, lont],
        cost=cost(4),
    )
    (parts,) = call(lat_block_kernel, "lat_block", [(lon, R // 2, 2 * m)], [got, y2])
    parts, b2, g2 = call(
        radial_modes_kernel, "radial_modes",
        [(lon, share * R, layers), (R, m), (R // 4, 4 * R)],
        [exchange(parts, "lon"), lp],
    )
    (parts,) = call(
        radial_sum_kernel, "radial_sum", [(lat, share * R + R // 4, layers)],
        [exchange(parts, "lon"), g2],
    )
    parts, g2 = call(
        radial_spread_kernel, "radial_spread", [(lon, share * R, layers), (R // 4, 4 * R)],
        [exchange(parts, "lat")],
    )
    got = exchange(parts, "lon")
    inv2, new_lat = call(
        lat_factor_kernel, "lat_factor", [(R, R), (m, R)], [g2, b2], cost=cost(4)
    )
    err, new_rad, core = call(
        functools.partial(last_kernel, m), "last",
        [(n * m, layers), (R, layers), (R * R, R)],
        [got.reshape(R * R, layers), inv2, new_lat, new_lon, wt, flat],
        scratch=[
            pltpu.VMEM((R * R, layers), jnp.float32),
            pltpu.VMEM((R * R, layers), jnp.float32),
            pltpu.VMEM((R * m, layers), jnp.float32),
        ],
    )
    return (t, err.reshape(n, m, layers), new_lon, new_lat, new_rad.T, core.reshape(R, R, R))


def solution(mesh):
    grid = P("lon", "lat", None)
    return jax.shard_map(
        local,
        mesh=mesh,
        in_specs=(grid, grid, grid, P("lon", None), P("lat", None), P()),
        out_specs=(grid, grid, P("lon", None), P("lat", None), P(), P()),
        check_vma=False,
    )
```

```python
import functools

import jax
import jax.numpy as jnp
from jax import lax
from jax.experimental import pallas as pl
from jax.experimental.pallas import tpu as pltpu
from jax.sharding import PartitionSpec as P

SHELL_LAYERS = 128
R = 32
STEPS = 4
time_step = 0.15
highest = lax.Precision.HIGHEST
W = STEPS


def dot(a, b, ca, cb):
    return lax.dot_general(
        a, b, (((ca,), (cb,)), ((), ())), precision=highest, preferred_element_type=jnp.float32
    )


def halves(x):
    high = x.astype(jnp.bfloat16)
    return high, (x - high.astype(jnp.float32)).astype(jnp.bfloat16)


def dot3(a, b, ca=1, cb=0):
    ah, al = halves(a) if not isinstance(a, tuple) else a
    bh, bl = halves(b) if not isinstance(b, tuple) else b

    def one(x, y):
        return lax.dot_general(
            x, y, (((ca,), (cb,)), ((), ())), preferred_element_type=jnp.float32
        )

    return one(ah, bh) + (one(ah, bl) + one(al, bh))


PAD = 4
TILE = PAD + W
SENT = 3 * W - 1


def pack_lat_kernel(t0, k0, s0, t1, k1, s1, low_ref, high_ref):
    n = t0.shape[0]
    for q in range(W):
        low_ref[q] = t0[:, q, :]
        low_ref[W + q] = k0[:, q, :]
        high_ref[q] = t1[:, TILE - W + q, :]
        high_ref[W + q] = k1[:, TILE - W + q, :]
    for q in range(W - 1):
        low_ref[2 * W + q] = s0[:, q, :]
        high_ref[2 * W + q] = s1[:, TILE - W + 1 + q, :]


def pack_lon_kernel(t0, k0, s0, t1, k1, s1, low_ref, high_ref):
    low_ref[0:W] = t0[...]
    low_ref[W:2 * W] = k0[...]
    low_ref[2 * W:] = s0[0:W - 1]
    high_ref[0:W] = t1[...]
    high_ref[W:2 * W] = k1[...]
    high_ref[2 * W:] = s1[1:W]


def pack(kernel, block, dim, t, k, s, slab, name):
    count = t.shape[dim] // block[dim]

    def spec(place):
        return pl.BlockSpec(block, lambda g: tuple(place if d == dim else 0 for d in range(3)))

    shape = jax.ShapeDtypeStruct((SENT,) + slab, jnp.float32)
    return pl.pallas_call(
        kernel,
        grid=(1,),
        out_shape=(shape, shape),
        in_specs=[spec(0)] * 3 + [spec(count - 1)] * 3,
        out_specs=[pl.BlockSpec(shape.shape, lambda g: (0, 0, 0))] * 2,
        name=name,
    )(t, k, s, t, k, s)


def face(p, q):
    summed = p + q
    return (2.0 * time_step) * p * q / jnp.where(summed > 0.0, summed, 1.0)


def conduct_kernel(n, m, lat, t_ref, k_ref, s_ref, below_ref, above_ref, south_ref, north_ref,
                   csouth_ref, cnorth_ref, v_ref, w_ref, out_ref, parts_ref,
                   ta, tb, k, s, hx, hy, hz, hd, full, z, sems):
    layers = t_ref.shape[2]
    planes = n + 2 * W
    end = TILE + m
    copies = [
        pltpu.make_async_copy(src, dst.at[W:n + W, TILE:end, :], sems.at[i])
        for i, (src, dst) in enumerate(((k_ref, k), (t_ref, ta), (s_ref, s)))
    ]
    for copy in copies:
        copy.start()
    for q in range(SENT):
        arr, at = ((ta, q), (k, q - W), (s, q - 2 * W))[q // W]
        late = q // W == 2
        low_row = PAD + at + (1 if late else 0)
        arr[W:n + W, low_row, :] = south_ref[q]
        arr[W:n + W, end + at, :] = north_ref[q]
        low_plane = at + (1 if late else 0)
        high_plane = n + W + at
        arr[low_plane, TILE:end, :] = below_ref[q]
        arr[high_plane, TILE:end, :] = above_ref[q]
        arr[low_plane, PAD:TILE, :] = csouth_ref[q, 0:W]
        arr[high_plane, PAD:TILE, :] = csouth_ref[q, W:2 * W]
        arr[low_plane, end:end + W, :] = cnorth_ref[q, 0:W]
        arr[high_plane, end:end + W, :] = cnorth_ref[q, W:2 * W]
    copies[0].wait()

    rows = slice(PAD, end + W)
    count = m + 2 * W
    inside = lax.broadcasted_iota(jnp.int32, (count, layers), 1) < layers - 1

    def faces(i, kc):
        kn = k[i + 1, rows, :]
        hx[i, rows, :] = face(kc, kn)
        hy[i, rows, :] = face(kc, k[i, PAD + 1:PAD + 1 + count, :])
        up = jnp.where(inside, face(kc, pltpu.roll(kc, layers - 1, 1)), 0.0)
        hz[i, rows, :] = up
        hd[i, rows, :] = pltpu.roll(up, 1, 1)
        return kn

    lax.fori_loop(0, planes - 1, faces, k[0, rows, :], unroll=4)

    copies[1].wait()
    copies[2].wait()
    for step in range(STEPS):
        last = step == STEPS - 1
        src, dst = (ta, tb) if step % 2 == 0 else (tb, ta)
        lo, num = (TILE, m) if last else (PAD, count)

        def body(p, carry):
            tc, before = carry
            tn = src[p + 1, lo:lo + num, :]
            fx = hx[p, lo:lo + num, :] * (tn - tc)
            fn = hy[p, lo:lo + num, :] * (src[p, lo + 1:lo + 1 + num, :] - tc)
            fs = hy[p, lo - 1:lo - 1 + num, :] * (src[p, lo - 1:lo - 1 + num, :] - tc)
            fu = hz[p, lo:lo + num, :] * (pltpu.roll(tc, layers - 1, 1) - tc)
            fd = hd[p, lo:lo + num, :] * (pltpu.roll(tc, 1, 1) - tc)
            gain = s[p, lo:lo + num, :]
            if step == 0:
                gain = gain * time_step
                s[p, lo:lo + num, :] = gain
            new = tc + ((gain + (fx - before)) + ((fn + fs) + (fu + fd)))
            if last:
                full[p - W] = new
            else:
                dst[p, lo:lo + num, :] = new
            return tn, fx

        tc = src[step + 1, lo:lo + num, :]
        start = hx[step, lo:lo + num, :] * (tc - src[step, lo:lo + num, :])
        lax.fori_loop(step + 1, planes - 1 - step, body, (tc, start), unroll=16)

    written = pltpu.make_async_copy(full, out_ref, sems.at[0])
    written.start()
    share = R // lat
    row = lax.broadcasted_iota(jnp.int32, (R, R), 0)
    col = lax.broadcasted_iota(jnp.int32, (R, R), 1)
    order = jnp.where(row % lat * share + row // lat == col, 1.0, 0.0).astype(jnp.float32)
    vh, vl = halves(dot(order, v_ref[...], 1, 0))
    lhs = jnp.concatenate([vh, vh, vl], axis=1)

    def project(i, c):
        pair = jnp.concatenate([full[2 * i], full[2 * i + 1]], axis=1)
        high, low = halves(pair)
        got = lax.dot_general(
            lhs, jnp.concatenate([high, low, high], axis=0), (((1,), (0,)), ((), ())),
            preferred_element_type=jnp.float32,
        )
        for e in range(2):
            for a in range(share):
                z[a, pl.ds(2 * i + e, lat, stride=n), :] = got[
                    a * lat:(a + 1) * lat, e * layers:(e + 1) * layers
                ]
        return c

    lax.fori_loop(0, n // 2, project, 0, unroll=4)
    tiled = jnp.concatenate([w_ref[...]] * share, axis=0)
    block = lax.broadcasted_iota(jnp.int32, tiled.shape, 0) // R
    total = None
    for a in range(share):
        part = dot3(z[a], jnp.where(block == a, tiled, 0.0), 1, 1)
        total = part if total is None else total + part
    parts_ref[...] = total
    written.wait()


def conduct(t, k, s, v, w):
    n, m, layers = t.shape
    lon, lat = lax.axis_size("lon"), lax.axis_size("lat")
    north_to = [(i, i + 1) for i in range(lat - 1)]
    south_to = [(j, i) for i, j in north_to]
    up = [(i, (i + 1) % lon) for i in range(lon)]
    down = [(j, i) for i, j in up]
    low, high = pack(pack_lat_kernel, (n, TILE, layers), 1, t, k, s, (n, layers), "pack_lat")
    south = lax.ppermute(high, "lat", north_to)
    north = lax.ppermute(low, "lat", south_to)
    low, high = pack(pack_lon_kernel, (W, m, layers), 0, t, k, s, (m, layers), "pack_lon")
    below = lax.ppermute(high, "lon", up)
    above = lax.ppermute(low, "lon", down)
    csouth = lax.ppermute(jnp.concatenate([below[:, m - W:], above[:, m - W:]], 1), "lat", north_to)
    cnorth = lax.ppermute(jnp.concatenate([below[:, :W], above[:, :W]], 1), "lat", south_to)
    share = R // lat
    big = pltpu.VMEM((n + 2 * W, m + 2 * TILE, layers), jnp.float32)
    vmem = pl.BlockSpec(memory_space=pltpu.VMEM)
    return pl.pallas_call(
        functools.partial(conduct_kernel, n, m, lat),
        out_shape=(
            jax.ShapeDtypeStruct(t.shape, jnp.float32),
            jax.ShapeDtypeStruct((lat * n, share * R), jnp.float32),
        ),
        in_specs=[pl.BlockSpec(memory_space=pl.ANY)] * 3 + [vmem] * 8,
        out_specs=[pl.BlockSpec(memory_space=pl.ANY), vmem],
        scratch_shapes=[big] * 8
        + [pltpu.VMEM(t.shape, jnp.float32), pltpu.VMEM((share, lat * n, layers), jnp.float32), pltpu.SemaphoreType.DMA((3,))],
        compiler_params=pltpu.CompilerParams(vmem_limit_bytes=56 * 2**20),
        name="conduct",
    )(t, k, s, below, above, south, north, csouth, cnorth, v.T, w.T)


def inverse_factor(gram):
    n = gram.shape[0]
    row = lax.broadcasted_iota(jnp.int32, (n, n), 0)
    inv = jnp.where(row == lax.broadcasted_iota(jnp.int32, (n, n), 1), 1.0, 0.0)
    scale = jnp.zeros((n, n), jnp.float32)
    columns = [jnp.broadcast_to(gram[:, k:k + 1], (n, n)) for k in range(n)]
    for j in range(n):
        top, at = j // 8 * 8, j % 8
        if at == 0 and j:
            columns = [c if c is None else c[8:] for c in columns]
        column = columns[j]
        pivot = column[at:at + 1]
        factor = jnp.where(row[top:] > j, column, 0.0) * (1.0 / pivot)
        for k in range(j + 1, n):
            columns[k] = columns[k] - factor * columns[k][at:at + 1]
        columns[j] = None
        scale = jnp.where(row == j, lax.rsqrt(pivot), scale)
        below = inv[top:] - factor * inv[j:j + 1]
        inv = below if top == 0 else jnp.concatenate([inv[:top], below], axis=0)
    return inv * scale


def call(kernel, name, outs, args, scratch=(), cost=None, aliases=None):
    vmem = pl.BlockSpec(memory_space=pltpu.VMEM)
    return pl.pallas_call(
        kernel,
        out_shape=tuple(jax.ShapeDtypeStruct(o, jnp.float32) for o in outs),
        in_specs=[vmem] * len(args),
        out_specs=(vmem,) * len(outs),
        scratch_shapes=list(scratch),
        compiler_params=pltpu.CompilerParams(vmem_limit_bytes=40 * 2**20),
        cost_estimate=cost,
        name=name,
    )(*args)


def cost(us):
    return pl.CostEstimate(flops=0, bytes_accessed=int(us * 3e6), transcendentals=0)


def add_up(ref):
    total = ref[0]
    for i in range(1, ref.shape[0]):
        total = total + ref[i]
    return total


def send_all(ref, x):
    for i in range(ref.shape[0]):
        ref[i] = x


def widen(x, n):
    k = x.shape[0] // n
    return jnp.concatenate([x[i * k:(i + 1) * k] for i in range(n)], axis=1)


def narrow(x, n):
    c = x.shape[1] // n
    return jnp.concatenate([x[:, i * c:(i + 1) * c] for i in range(n)], axis=0)


def eye(n):
    row = lax.broadcasted_iota(jnp.int32, (n, n), 0)
    return jnp.where(row == lax.broadcasted_iota(jnp.int32, (n, n), 1), 1.0, 0.0).astype(jnp.float32)


def flip(x):
    return dot(eye(x.shape[1]), x, 1, 1)


def diagonal(x, n):
    k = x.shape[0]
    wide = jnp.concatenate([x] * n, axis=1)
    wide = jnp.concatenate([wide] * n, axis=0)
    row = lax.broadcasted_iota(jnp.int32, wide.shape, 0) // k
    col = lax.broadcasted_iota(jnp.int32, wide.shape, 1) // k
    return jnp.where(row == col, wide, 0.0)


def stack_left(x):
    high, low = halves(x)
    return jnp.concatenate([high, high, low], axis=1)


def stack_right(x):
    high, low = halves(x)
    return jnp.concatenate([high, low, high], axis=0)


def product(left, right):
    return lax.dot_general(
        left, right, (((1,), (0,)), ((), ())), preferred_element_type=jnp.float32
    )


def lon_project_kernel(got, ut, y1, out):
    y = add_up(got)
    y1[...] = y
    send_all(out, dot(ut[...], y, 1, 0))


def lon_block_kernel(got, y1, out):
    send_all(out, widen(dot(add_up(got), y1[...], 1, 1), 2))


def radial_kernel(m, t, wt, out):
    n = t.shape[0] // m
    half = m // 2
    share = out.shape[0]
    peers = R // share
    w = halves(wt[...])

    def body(j, c):
        x = jnp.concatenate(
            [t[pl.ds(j + h * half, n, stride=m), :] for h in range(2)], axis=0
        )
        got = dot3(w, x, 1, 1)
        for b in range(share):
            out[b, pl.ds(j, peers, stride=half), :] = got[b * peers:(b + 1) * peers]
        return c

    lax.fori_loop(0, half, body, 0, unroll=4)


def lat_modes_kernel(got, rt, out, b1):
    block = narrow(add_up(got), 2)
    b1[...] = block
    gram = widen(dot(block, block, 1, 1), 4)
    wide = jnp.concatenate([block, block], axis=1)
    wide = jnp.concatenate([wide] * 4, axis=0)
    row = lax.broadcasted_iota(jnp.int32, wide.shape, 0) // R
    half = lax.broadcasted_iota(jnp.int32, wide.shape, 1) // block.shape[1]
    total = None
    for b in range(rt.shape[0]):
        part = dot3(rt[b], jnp.where(row == 2 * b + half, wide, 0.0), 1, 1)
        total = part if total is None else total + part
    rows = total.shape[0] // out.shape[0]
    for i in range(out.shape[0]):
        out[i, 0:rows] = total[i * rows:(i + 1) * rows]
        out[i, rows:] = gram


def lat_project_kernel(got, b1, vt, out, y2, lon, lont):
    total = add_up(got)
    gram = narrow(total[total.shape[0] - R // 4:], 4)
    inv = inverse_factor(gram)
    block = b1[...]
    lont[...] = dot(inv, block, 1, 0)
    lon[...] = dot(flip(block), inv, 1, 1)
    y = dot(total[:total.shape[0] - R // 4], diagonal(inv, 4), 1, 1)
    y2[...] = y
    half = vt.shape[1] // 2
    lane = lax.broadcasted_iota(jnp.int32, (R, y.shape[1]), 1) // R % 2
    send_all(
        out,
        jnp.where(
            lane == 0, dot(vt[:, 0:half], y, 1, 0), dot(vt[:, half:], y, 1, 0)
        ),
    )


def lon_sums_kernel(m, t, lont, out):
    n = t.shape[0] // m
    layers = t.shape[1]
    left = stack_left(lont[...])

    def body(j, c):
        x = jnp.concatenate([t[pl.ds(2 * j + e, n, stride=m), :] for e in range(2)], axis=1)
        got = product(left, stack_right(x))
        for e in range(2):
            out[pl.ds(2 * j + e, R, stride=m), :] = got[:, e * layers:(e + 1) * layers]
        return c

    lax.fori_loop(0, m // 2, body, 0, unroll=4)


def lat_block_kernel(got, y2, out):
    q = add_up(got)
    y = y2[...]
    lane = lax.broadcasted_iota(jnp.int32, q.shape, 1) // R % 2
    width = q.shape[1]
    both = q + jnp.where(lane == 0, pltpu.roll(q, width - R, 1), pltpu.roll(q, R, 1))
    side = lax.broadcasted_iota(jnp.int32, y.shape, 1) // R % 2
    rows = jnp.concatenate([jnp.where(side == 0, y, 0.0), jnp.where(side == 1, y, 0.0)], axis=0)
    send_all(out, widen(dot(both, rows, 1, 1), 2))


def radial_modes_kernel(got, lp, out, b2, g2):
    block = narrow(add_up(got), 2)
    b2[...] = block
    g2[...] = widen(dot(block, block, 1, 1), 4)
    left = stack_left(block)
    m = block.shape[1]
    layers = lp.shape[1]

    def body(a, c):
        x = jnp.concatenate(
            [lp[pl.ds(pl.multiple_of((2 * a + e) * m, m), m), :] for e in range(2)], axis=1
        )
        y = product(left, stack_right(x))
        for e in range(2):
            out[a, e * R:(e + 1) * R, :] = y[:, e * layers:(e + 1) * layers]
        return c

    lax.fori_loop(0, R // 2, body, 0, unroll=4)


def radial_sum_kernel(got, g2, out):
    total = add_up(got)
    for i in range(out.shape[0]):
        out[i, 0:total.shape[0]] = total
        out[i, total.shape[0]:] = g2[...]


def radial_spread_kernel(got, out, g2):
    total = add_up(got)
    rows = out.shape[1]
    send_all(out, total[:rows])
    g2[...] = total[rows:]


def lat_factor_kernel(g2, b2, inv, lat):
    inverse = inverse_factor(narrow(g2[...], 4))
    inv[...] = inverse
    lat[...] = dot(flip(b2[...]), inverse, 1, 1)


def last_kernel(m, y3_ref, inv2, lat, lon, wt, t, err, rad, core_ref, y3, first, second):
    layers = y3.shape[1]
    n = t.shape[0] // m
    mix = halves(diagonal(inv2[...], layers // R))
    for i in range(y3.shape[0] // layers):
        y3[i * layers:(i + 1) * layers] = dot3(mix, y3_ref[i * layers:(i + 1) * layers])
    y = halves(y3[...])
    proj = dot3(wt[...], y, 1, 1)
    block = dot3(proj, y)
    inv = inverse_factor(dot(block, block, 1, 1))
    radt = dot(inv, block, 1, 0)
    rad[...] = radt
    radh = halves(radt)
    core = dot3(y, radh, 1, 1)
    core_ref[...] = core
    first[...] = dot3(core, radh)
    left = stack_left(lat[...])

    def widen_lat(a, c):
        x = jnp.concatenate(
            [first[pl.ds(pl.multiple_of((2 * a + e) * R, R), R), :] for e in range(2)], axis=1
        )
        got = product(left, stack_right(x))
        for e in range(2):
            at = pl.multiple_of((2 * a + e) * m, m)
            second[pl.ds(at, m), :] = got[:, e * layers:(e + 1) * layers]
        return c

    lax.fori_loop(0, R // 2, widen_lat, 0, unroll=4)
    lonl = stack_left(lon[...])

    def widen_lon(j, c):
        x = jnp.concatenate(
            [second[pl.ds(2 * j + e, R, stride=m), :] for e in range(2)], axis=1
        )
        got = product(lonl, stack_right(x))
        for e in range(2):
            at = pl.ds(2 * j + e, n, stride=m)
            err[at, :] = t[at, :] - got[:, e * layers:(e + 1) * layers]
        return c

    lax.fori_loop(0, m // 2, widen_lon, 0, unroll=4)


def exchange(parts, axis):
    return lax.all_to_all(parts, axis, 0, 0, tiled=True)


def local(t0, k, s, u, v, w):
    n, m, layers = t0.shape
    lon, lat = lax.axis_size("lon"), lax.axis_size("lat")
    t, parts = conduct(t0, k, s, v, w)
    flat = t.reshape(n * m, layers)
    share = R // lon
    wt = w.T
    vt = v.T
    wide = R // lat * R
    got = exchange(parts.reshape(lat, n, wide), "lat")
    (rt,) = call(
        functools.partial(radial_kernel, m), "radial",
        [(share, lon * m // 2, 2 * n)],
        [flat, wt.reshape(lon, share, layers).transpose(1, 0, 2).reshape(R, layers)],
        cost=cost(4),
    )
    y1, parts = call(
        lon_project_kernel, "lon_project", [(n, wide), (lon, R, wide)], [got, u.T]
    )
    (parts,) = call(
        lon_block_kernel, "lon_block", [(lat, R // 2, 2 * n)], [exchange(parts, "lon"), y1]
    )
    parts, b1 = call(
        lat_modes_kernel, "lat_modes", [(lon, m // 2 + R // 4, 2 * share * R), (R, n)],
        [exchange(parts, "lat"), rt],
    )
    parts, y2, new_lon, lont = call(
        lat_project_kernel, "lat_project",
        [(lat, R, 2 * share * R), (m // 2, 2 * share * R), (n, R), (R, n)],
        [exchange(parts, "lon"), b1, vt],
    )
    got = exchange(parts, "lat")
    (lp,) = call(
        functools.partial(lon_sums_kernel, m), "lon_sums", [(R * m, layers)], [flat, lont],
        cost=cost(4),
    )
    (parts,) = call(lat_block_kernel, "lat_block", [(lon, R // 2, 2 * m)], [got, y2])
    parts, b2, g2 = call(
        radial_modes_kernel, "radial_modes",
        [(lon, share * R, layers), (R, m), (R // 4, 4 * R)],
        [exchange(parts, "lon"), lp],
    )
    (parts,) = call(
        radial_sum_kernel, "radial_sum", [(lat, share * R + R // 4, layers)],
        [exchange(parts, "lon"), g2],
    )
    parts, g2 = call(
        radial_spread_kernel, "radial_spread", [(lon, share * R, layers), (R // 4, 4 * R)],
        [exchange(parts, "lat")],
    )
    got = exchange(parts, "lon")
    inv2, new_lat = call(
        lat_factor_kernel, "lat_factor", [(R, R), (m, R)], [g2, b2], cost=cost(4)
    )
    err, new_rad, core = call(
        functools.partial(last_kernel, m), "last",
        [(n * m, layers), (R, layers), (R * R, R)],
        [got.reshape(R * R, layers), inv2, new_lat, new_lon, wt, flat],
        scratch=[
            pltpu.VMEM((R * R, layers), jnp.float32),
            pltpu.VMEM((R * R, layers), jnp.float32),
            pltpu.VMEM((R * m, layers), jnp.float32),
        ],
    )
    return (t, err.reshape(n, m, layers), new_lon, new_lat, new_rad.T, core.reshape(R, R, R))


def solution(mesh):
    grid = P("lon", "lat", None)
    return jax.shard_map(
        local,
        mesh=mesh,
        in_specs=(grid, grid, grid, P("lon", None), P("lat", None), P()),
        out_specs=(grid, grid, P("lon", None), P("lat", None), P(), P()),
        check_vma=False,
    )
```

```python
import functools

import jax
import jax.numpy as jnp
from jax import lax
from jax.experimental import pallas as pl
from jax.experimental.pallas import tpu as pltpu
from jax.sharding import PartitionSpec as P

SHELL_LAYERS = 128
R = 32
STEPS = 4
time_step = 0.15
highest = lax.Precision.HIGHEST
W = STEPS


def dot(a, b, ca, cb):
    return lax.dot_general(
        a, b, (((ca,), (cb,)), ((), ())), precision=highest, preferred_element_type=jnp.float32
    )


def halves(x):
    high = x.astype(jnp.bfloat16)
    return high, (x - high.astype(jnp.float32)).astype(jnp.bfloat16)


def dot3(a, b, ca=1, cb=0):
    ah, al = halves(a) if not isinstance(a, tuple) else a
    bh, bl = halves(b) if not isinstance(b, tuple) else b

    def one(x, y):
        return lax.dot_general(
            x, y, (((ca,), (cb,)), ((), ())), preferred_element_type=jnp.float32
        )

    return one(ah, bh) + (one(ah, bl) + one(al, bh))


PAD = 4
TILE = PAD + W
SENT = 3 * W - 1


def pack_lat_kernel(t0, k0, s0, t1, k1, s1, low_ref, high_ref):
    n = t0.shape[0]
    for q in range(W):
        low_ref[q] = t0[:, q, :]
        low_ref[W + q] = k0[:, q, :]
        high_ref[q] = t1[:, TILE - W + q, :]
        high_ref[W + q] = k1[:, TILE - W + q, :]
    for q in range(W - 1):
        low_ref[2 * W + q] = s0[:, q, :]
        high_ref[2 * W + q] = s1[:, TILE - W + 1 + q, :]


def pack_lon_kernel(t0, k0, s0, t1, k1, s1, low_ref, high_ref):
    low_ref[0:W] = t0[...]
    low_ref[W:2 * W] = k0[...]
    low_ref[2 * W:] = s0[0:W - 1]
    high_ref[0:W] = t1[...]
    high_ref[W:2 * W] = k1[...]
    high_ref[2 * W:] = s1[1:W]


def pack(kernel, block, dim, t, k, s, slab, name):
    count = t.shape[dim] // block[dim]

    def spec(place):
        return pl.BlockSpec(block, lambda g: tuple(place if d == dim else 0 for d in range(3)))

    shape = jax.ShapeDtypeStruct((SENT,) + slab, jnp.float32)
    return pl.pallas_call(
        kernel,
        grid=(1,),
        out_shape=(shape, shape),
        in_specs=[spec(0)] * 3 + [spec(count - 1)] * 3,
        out_specs=[pl.BlockSpec(shape.shape, lambda g: (0, 0, 0))] * 2,
        name=name,
    )(t, k, s, t, k, s)


def face(p, q):
    summed = p + q
    return (2.0 * time_step) * p * q / jnp.where(summed > 0.0, summed, 1.0)


def conduct_kernel(n, m, lat, t_ref, k_ref, s_ref, below_ref, above_ref, south_ref, north_ref,
                   csouth_ref, cnorth_ref, v_ref, w_ref, out_ref, parts_ref,
                   ta, tb, k, s, hx, hy, hz, hd, full, z, sems):
    layers = t_ref.shape[2]
    planes = n + 2 * W
    end = TILE + m
    copies = [
        pltpu.make_async_copy(src, dst.at[W:n + W, TILE:end, :], sems.at[i])
        for i, (src, dst) in enumerate(((k_ref, k), (t_ref, ta), (s_ref, s)))
    ]
    for copy in copies:
        copy.start()
    for q in range(SENT):
        arr, at = ((ta, q), (k, q - W), (s, q - 2 * W))[q // W]
        late = q // W == 2
        low_row = PAD + at + (1 if late else 0)
        arr[W:n + W, low_row, :] = south_ref[q]
        arr[W:n + W, end + at, :] = north_ref[q]
        low_plane = at + (1 if late else 0)
        high_plane = n + W + at
        arr[low_plane, TILE:end, :] = below_ref[q]
        arr[high_plane, TILE:end, :] = above_ref[q]
        arr[low_plane, PAD:TILE, :] = csouth_ref[q, 0:W]
        arr[high_plane, PAD:TILE, :] = csouth_ref[q, W:2 * W]
        arr[low_plane, end:end + W, :] = cnorth_ref[q, 0:W]
        arr[high_plane, end:end + W, :] = cnorth_ref[q, W:2 * W]
    copies[0].wait()

    rows = slice(PAD, end + W)
    count = m + 2 * W
    inside = lax.broadcasted_iota(jnp.int32, (count, layers), 1) < layers - 1

    def faces(i, kc):
        kn = k[i + 1, rows, :]
        hx[i, rows, :] = face(kc, kn)
        hy[i, rows, :] = face(kc, k[i, PAD + 1:PAD + 1 + count, :])
        up = jnp.where(inside, face(kc, pltpu.roll(kc, layers - 1, 1)), 0.0)
        hz[i, rows, :] = up
        hd[i, rows, :] = pltpu.roll(up, 1, 1)
        return kn

    lax.fori_loop(0, planes - 1, faces, k[0, rows, :], unroll=8)

    copies[1].wait()
    copies[2].wait()
    for step in range(STEPS):
        last = step == STEPS - 1
        src, dst = (ta, tb) if step % 2 == 0 else (tb, ta)
        lo, num = (TILE, m) if last else (PAD, count)

        def body(p, carry):
            tc, before = carry
            tn = src[p + 1, lo:lo + num, :]
            fx = hx[p, lo:lo + num, :] * (tn - tc)
            fn = hy[p, lo:lo + num, :] * (src[p, lo + 1:lo + 1 + num, :] - tc)
            fs = hy[p, lo - 1:lo - 1 + num, :] * (src[p, lo - 1:lo - 1 + num, :] - tc)
            fu = hz[p, lo:lo + num, :] * (pltpu.roll(tc, layers - 1, 1) - tc)
            fd = hd[p, lo:lo + num, :] * (pltpu.roll(tc, 1, 1) - tc)
            gain = s[p, lo:lo + num, :]
            if step == 0:
                gain = gain * time_step
                s[p, lo:lo + num, :] = gain
            new = tc + ((gain + (fx - before)) + ((fn + fs) + (fu + fd)))
            if last:
                full[p - W] = new
            else:
                dst[p, lo:lo + num, :] = new
            return tn, fx

        tc = src[step + 1, lo:lo + num, :]
        start = hx[step, lo:lo + num, :] * (tc - src[step, lo:lo + num, :])
        lax.fori_loop(step + 1, planes - 1 - step, body, (tc, start), unroll=16)

    written = pltpu.make_async_copy(full, out_ref, sems.at[0])
    written.start()
    share = R // lat
    row = lax.broadcasted_iota(jnp.int32, (R, R), 0)
    col = lax.broadcasted_iota(jnp.int32, (R, R), 1)
    order = jnp.where(row % lat * share + row // lat == col, 1.0, 0.0).astype(jnp.float32)
    vh, vl = halves(dot(order, v_ref[...], 1, 0))
    lhs = jnp.concatenate([vh, vh, vl], axis=1)

    def project(i, c):
        pair = jnp.concatenate([full[2 * i], full[2 * i + 1]], axis=1)
        high, low = halves(pair)
        got = lax.dot_general(
            lhs, jnp.concatenate([high, low, high], axis=0), (((1,), (0,)), ((), ())),
            preferred_element_type=jnp.float32,
        )
        for e in range(2):
            for a in range(share):
                z[a, pl.ds(2 * i + e, lat, stride=n), :] = got[
                    a * lat:(a + 1) * lat, e * layers:(e + 1) * layers
                ]
        return c

    lax.fori_loop(0, n // 2, project, 0, unroll=8)
    tiled = jnp.concatenate([w_ref[...]] * share, axis=0)
    block = lax.broadcasted_iota(jnp.int32, tiled.shape, 0) // R
    total = None
    for a in range(share):
        part = dot3(z[a], jnp.where(block == a, tiled, 0.0), 1, 1)
        total = part if total is None else total + part
    parts_ref[...] = total
    written.wait()


def conduct(t, k, s, v, w):
    n, m, layers = t.shape
    lon, lat = lax.axis_size("lon"), lax.axis_size("lat")
    north_to = [(i, i + 1) for i in range(lat - 1)]
    south_to = [(j, i) for i, j in north_to]
    up = [(i, (i + 1) % lon) for i in range(lon)]
    down = [(j, i) for i, j in up]
    low, high = pack(pack_lat_kernel, (n, TILE, layers), 1, t, k, s, (n, layers), "pack_lat")
    south = lax.ppermute(high, "lat", north_to)
    north = lax.ppermute(low, "lat", south_to)
    low, high = pack(pack_lon_kernel, (W, m, layers), 0, t, k, s, (m, layers), "pack_lon")
    below = lax.ppermute(high, "lon", up)
    above = lax.ppermute(low, "lon", down)
    csouth = lax.ppermute(jnp.concatenate([below[:, m - W:], above[:, m - W:]], 1), "lat", north_to)
    cnorth = lax.ppermute(jnp.concatenate([below[:, :W], above[:, :W]], 1), "lat", south_to)
    share = R // lat
    big = pltpu.VMEM((n + 2 * W, m + 2 * TILE, layers), jnp.float32)
    vmem = pl.BlockSpec(memory_space=pltpu.VMEM)
    return pl.pallas_call(
        functools.partial(conduct_kernel, n, m, lat),
        out_shape=(
            jax.ShapeDtypeStruct(t.shape, jnp.float32),
            jax.ShapeDtypeStruct((lat * n, share * R), jnp.float32),
        ),
        in_specs=[pl.BlockSpec(memory_space=pl.ANY)] * 3 + [vmem] * 8,
        out_specs=[pl.BlockSpec(memory_space=pl.ANY), vmem],
        scratch_shapes=[big] * 8
        + [pltpu.VMEM(t.shape, jnp.float32), pltpu.VMEM((share, lat * n, layers), jnp.float32), pltpu.SemaphoreType.DMA((3,))],
        compiler_params=pltpu.CompilerParams(vmem_limit_bytes=56 * 2**20),
        name="conduct",
    )(t, k, s, below, above, south, north, csouth, cnorth, v.T, w.T)


def inverse_factor(gram):
    n = gram.shape[0]
    row = lax.broadcasted_iota(jnp.int32, (n, n), 0)
    inv = jnp.where(row == lax.broadcasted_iota(jnp.int32, (n, n), 1), 1.0, 0.0)
    scale = jnp.zeros((n, n), jnp.float32)
    columns = [jnp.broadcast_to(gram[:, k:k + 1], (n, n)) for k in range(n)]
    for j in range(n):
        top, at = j // 8 * 8, j % 8
        if at == 0 and j:
            columns = [c if c is None else c[8:] for c in columns]
        column = columns[j]
        pivot = column[at:at + 1]
        factor = jnp.where(row[top:] > j, column, 0.0) * (1.0 / pivot)
        for k in range(j + 1, n):
            columns[k] = columns[k] - factor * columns[k][at:at + 1]
        columns[j] = None
        scale = jnp.where(row == j, lax.rsqrt(pivot), scale)
        below = inv[top:] - factor * inv[j:j + 1]
        inv = below if top == 0 else jnp.concatenate([inv[:top], below], axis=0)
    return inv * scale


def call(kernel, name, outs, args, scratch=(), cost=None, aliases=None):
    vmem = pl.BlockSpec(memory_space=pltpu.VMEM)
    return pl.pallas_call(
        kernel,
        out_shape=tuple(jax.ShapeDtypeStruct(o, jnp.float32) for o in outs),
        in_specs=[vmem] * len(args),
        out_specs=(vmem,) * len(outs),
        scratch_shapes=list(scratch),
        compiler_params=pltpu.CompilerParams(vmem_limit_bytes=40 * 2**20),
        cost_estimate=cost,
        name=name,
    )(*args)


def cost(us):
    return pl.CostEstimate(flops=0, bytes_accessed=int(us * 3e6), transcendentals=0)


def add_up(ref):
    total = ref[0]
    for i in range(1, ref.shape[0]):
        total = total + ref[i]
    return total


def send_all(ref, x):
    for i in range(ref.shape[0]):
        ref[i] = x


def widen(x, n):
    k = x.shape[0] // n
    return jnp.concatenate([x[i * k:(i + 1) * k] for i in range(n)], axis=1)


def narrow(x, n):
    c = x.shape[1] // n
    return jnp.concatenate([x[:, i * c:(i + 1) * c] for i in range(n)], axis=0)


def eye(n):
    row = lax.broadcasted_iota(jnp.int32, (n, n), 0)
    return jnp.where(row == lax.broadcasted_iota(jnp.int32, (n, n), 1), 1.0, 0.0).astype(jnp.float32)


def flip(x):
    return dot(eye(x.shape[1]), x, 1, 1)


def diagonal(x, n):
    k = x.shape[0]
    wide = jnp.concatenate([x] * n, axis=1)
    wide = jnp.concatenate([wide] * n, axis=0)
    row = lax.broadcasted_iota(jnp.int32, wide.shape, 0) // k
    col = lax.broadcasted_iota(jnp.int32, wide.shape, 1) // k
    return jnp.where(row == col, wide, 0.0)


def stack_left(x):
    high, low = halves(x)
    return jnp.concatenate([high, high, low], axis=1)


def stack_right(x):
    high, low = halves(x)
    return jnp.concatenate([high, low, high], axis=0)


def product(left, right):
    return lax.dot_general(
        left, right, (((1,), (0,)), ((), ())), preferred_element_type=jnp.float32
    )


def lon_project_kernel(got, ut, y1, out):
    y = add_up(got)
    y1[...] = y
    send_all(out, dot(ut[...], y, 1, 0))


def lon_block_kernel(got, y1, out):
    send_all(out, widen(dot(add_up(got), y1[...], 1, 1), 2))


def radial_kernel(m, t, wt, out):
    n = t.shape[0] // m
    half = m // 2
    share = out.shape[0]
    peers = R // share
    w = halves(wt[...])

    def body(j, c):
        x = jnp.concatenate(
            [t[pl.ds(j + h * half, n, stride=m), :] for h in range(2)], axis=0
        )
        got = dot3(w, x, 1, 1)
        for b in range(share):
            out[b, pl.ds(j, peers, stride=half), :] = got[b * peers:(b + 1) * peers]
        return c

    lax.fori_loop(0, half, body, 0, unroll=4)


def lat_modes_kernel(got, rt, out, b1):
    block = narrow(add_up(got), 2)
    b1[...] = block
    gram = widen(dot(block, block, 1, 1), 4)
    wide = jnp.concatenate([block, block], axis=1)
    wide = jnp.concatenate([wide] * 4, axis=0)
    row = lax.broadcasted_iota(jnp.int32, wide.shape, 0) // R
    half = lax.broadcasted_iota(jnp.int32, wide.shape, 1) // block.shape[1]
    total = None
    for b in range(rt.shape[0]):
        part = dot3(rt[b], jnp.where(row == 2 * b + half, wide, 0.0), 1, 1)
        total = part if total is None else total + part
    rows = total.shape[0] // out.shape[0]
    for i in range(out.shape[0]):
        out[i, 0:rows] = total[i * rows:(i + 1) * rows]
        out[i, rows:] = gram


def lat_project_kernel(got, b1, vt, out, y2, lon, lont):
    total = add_up(got)
    gram = narrow(total[total.shape[0] - R // 4:], 4)
    inv = inverse_factor(gram)
    block = b1[...]
    lont[...] = dot(inv, block, 1, 0)
    lon[...] = dot(flip(block), inv, 1, 1)
    y = dot(total[:total.shape[0] - R // 4], diagonal(inv, 4), 1, 1)
    y2[...] = y
    half = vt.shape[1] // 2
    lane = lax.broadcasted_iota(jnp.int32, (R, y.shape[1]), 1) // R % 2
    send_all(
        out,
        jnp.where(
            lane == 0, dot(vt[:, 0:half], y, 1, 0), dot(vt[:, half:], y, 1, 0)
        ),
    )


def lon_sums_kernel(m, t, lont, out):
    n = t.shape[0] // m
    layers = t.shape[1]
    left = stack_left(lont[...])

    def body(j, c):
        x = jnp.concatenate([t[pl.ds(2 * j + e, n, stride=m), :] for e in range(2)], axis=1)
        got = product(left, stack_right(x))
        for e in range(2):
            out[pl.ds(2 * j + e, R, stride=m), :] = got[:, e * layers:(e + 1) * layers]
        return c

    lax.fori_loop(0, m // 2, body, 0, unroll=4)


def lat_block_kernel(got, y2, out):
    q = add_up(got)
    y = y2[...]
    lane = lax.broadcasted_iota(jnp.int32, q.shape, 1) // R % 2
    width = q.shape[1]
    both = q + jnp.where(lane == 0, pltpu.roll(q, width - R, 1), pltpu.roll(q, R, 1))
    side = lax.broadcasted_iota(jnp.int32, y.shape, 1) // R % 2
    rows = jnp.concatenate([jnp.where(side == 0, y, 0.0), jnp.where(side == 1, y, 0.0)], axis=0)
    send_all(out, widen(dot(both, rows, 1, 1), 2))


def radial_modes_kernel(got, lp, out, b2, g2):
    block = narrow(add_up(got), 2)
    b2[...] = block
    g2[...] = widen(dot(block, block, 1, 1), 4)
    left = stack_left(block)
    m = block.shape[1]
    layers = lp.shape[1]

    def body(a, c):
        x = jnp.concatenate(
            [lp[pl.ds(pl.multiple_of((2 * a + e) * m, m), m), :] for e in range(2)], axis=1
        )
        y = product(left, stack_right(x))
        for e in range(2):
            out[a, e * R:(e + 1) * R, :] = y[:, e * layers:(e + 1) * layers]
        return c

    lax.fori_loop(0, R // 2, body, 0, unroll=16)


def radial_sum_kernel(got, g2, out):
    total = add_up(got)
    for i in range(out.shape[0]):
        out[i, 0:total.shape[0]] = total
        out[i, total.shape[0]:] = g2[...]


def radial_spread_kernel(got, out, g2):
    total = add_up(got)
    rows = out.shape[1]
    send_all(out, total[:rows])
    g2[...] = total[rows:]


def lat_factor_kernel(g2, b2, inv, lat):
    inverse = inverse_factor(narrow(g2[...], 4))
    inv[...] = inverse
    lat[...] = dot(flip(b2[...]), inverse, 1, 1)


def last_kernel(m, y3_ref, inv2, lat, lon, wt, t, err, rad, core_ref, y3, first, second):
    layers = y3.shape[1]
    n = t.shape[0] // m
    mix = halves(diagonal(inv2[...], layers // R))
    for i in range(y3.shape[0] // layers):
        y3[i * layers:(i + 1) * layers] = dot3(mix, y3_ref[i * layers:(i + 1) * layers])
    y = halves(y3[...])
    proj = dot3(wt[...], y, 1, 1)
    block = dot3(proj, y)
    inv = inverse_factor(dot(block, block, 1, 1))
    radt = dot(inv, block, 1, 0)
    rad[...] = radt
    radh = halves(radt)
    core = dot3(y, radh, 1, 1)
    core_ref[...] = core
    first[...] = dot3(core, radh)
    left = stack_left(lat[...])

    def widen_lat(a, c):
        x = jnp.concatenate(
            [first[pl.ds(pl.multiple_of((2 * a + e) * R, R), R), :] for e in range(2)], axis=1
        )
        got = product(left, stack_right(x))
        for e in range(2):
            at = pl.multiple_of((2 * a + e) * m, m)
            second[pl.ds(at, m), :] = got[:, e * layers:(e + 1) * layers]
        return c

    lax.fori_loop(0, R // 2, widen_lat, 0, unroll=16)
    lonl = stack_left(lon[...])

    def widen_lon(j, c):
        x = jnp.concatenate(
            [second[pl.ds(2 * j + e, R, stride=m), :] for e in range(2)], axis=1
        )
        got = product(lonl, stack_right(x))
        for e in range(2):
            at = pl.ds(2 * j + e, n, stride=m)
            err[at, :] = t[at, :] - got[:, e * layers:(e + 1) * layers]
        return c

    lax.fori_loop(0, m // 2, widen_lon, 0, unroll=16)


def exchange(parts, axis):
    return lax.all_to_all(parts, axis, 0, 0, tiled=True)


def local(t0, k, s, u, v, w):
    n, m, layers = t0.shape
    lon, lat = lax.axis_size("lon"), lax.axis_size("lat")
    t, parts = conduct(t0, k, s, v, w)
    flat = t.reshape(n * m, layers)
    share = R // lon
    wt = w.T
    vt = v.T
    wide = R // lat * R
    got = exchange(parts.reshape(lat, n, wide), "lat")
    (rt,) = call(
        functools.partial(radial_kernel, m), "radial",
        [(share, lon * m // 2, 2 * n)],
        [flat, wt.reshape(lon, share, layers).transpose(1, 0, 2).reshape(R, layers)],
        cost=cost(4),
    )
    y1, parts = call(
        lon_project_kernel, "lon_project", [(n, wide), (lon, R, wide)], [got, u.T]
    )
    (parts,) = call(
        lon_block_kernel, "lon_block", [(lat, R // 2, 2 * n)], [exchange(parts, "lon"), y1]
    )
    parts, b1 = call(
        lat_modes_kernel, "lat_modes", [(lon, m // 2 + R // 4, 2 * share * R), (R, n)],
        [exchange(parts, "lat"), rt],
    )
    parts, y2, new_lon, lont = call(
        lat_project_kernel, "lat_project",
        [(lat, R, 2 * share * R), (m // 2, 2 * share * R), (n, R), (R, n)],
        [exchange(parts, "lon"), b1, vt],
    )
    got = exchange(parts, "lat")
    (lp,) = call(
        functools.partial(lon_sums_kernel, m), "lon_sums", [(R * m, layers)], [flat, lont],
        cost=cost(4),
    )
    (parts,) = call(lat_block_kernel, "lat_block", [(lon, R // 2, 2 * m)], [got, y2])
    parts, b2, g2 = call(
        radial_modes_kernel, "radial_modes",
        [(lon, share * R, layers), (R, m), (R // 4, 4 * R)],
        [exchange(parts, "lon"), lp],
    )
    (parts,) = call(
        radial_sum_kernel, "radial_sum", [(lat, share * R + R // 4, layers)],
        [exchange(parts, "lon"), g2],
    )
    parts, g2 = call(
        radial_spread_kernel, "radial_spread", [(lon, share * R, layers), (R // 4, 4 * R)],
        [exchange(parts, "lat")],
    )
    got = exchange(parts, "lon")
    inv2, new_lat = call(
        lat_factor_kernel, "lat_factor", [(R, R), (m, R)], [g2, b2], cost=cost(4)
    )
    err, new_rad, core = call(
        functools.partial(last_kernel, m), "last",
        [(n * m, layers), (R, layers), (R * R, R)],
        [got.reshape(R * R, layers), inv2, new_lat, new_lon, wt, flat],
        scratch=[
            pltpu.VMEM((R * R, layers), jnp.float32),
            pltpu.VMEM((R * R, layers), jnp.float32),
            pltpu.VMEM((R * m, layers), jnp.float32),
        ],
    )
    return (t, err.reshape(n, m, layers), new_lon, new_lat, new_rad.T, core.reshape(R, R, R))


def solution(mesh):
    grid = P("lon", "lat", None)
    return jax.shard_map(
        local,
        mesh=mesh,
        in_specs=(grid, grid, grid, P("lon", None), P("lat", None), P()),
        out_specs=(grid, grid, P("lon", None), P("lat", None), P(), P()),
        check_vma=False,
    )
```

```python
import functools

import jax
import jax.numpy as jnp
from jax import lax
from jax.experimental import pallas as pl
from jax.experimental.pallas import tpu as pltpu
from jax.sharding import PartitionSpec as P

SHELL_LAYERS = 128
R = 32
STEPS = 4
time_step = 0.15
highest = lax.Precision.HIGHEST
W = STEPS


def dot(a, b, ca, cb):
    return lax.dot_general(
        a, b, (((ca,), (cb,)), ((), ())), precision=highest, preferred_element_type=jnp.float32
    )


def halves(x):
    high = x.astype(jnp.bfloat16)
    return high, (x - high.astype(jnp.float32)).astype(jnp.bfloat16)


def dot3(a, b, ca=1, cb=0):
    ah, al = halves(a) if not isinstance(a, tuple) else a
    bh, bl = halves(b) if not isinstance(b, tuple) else b

    def one(x, y):
        return lax.dot_general(
            x, y, (((ca,), (cb,)), ((), ())), preferred_element_type=jnp.float32
        )

    return one(ah, bh) + (one(ah, bl) + one(al, bh))


PAD = 4
TILE = PAD + W
SENT = 3 * W - 1


def pack_lat_kernel(t0, k0, s0, t1, k1, s1, low_ref, high_ref):
    n = t0.shape[0]
    for q in range(W):
        low_ref[q] = t0[:, q, :]
        low_ref[W + q] = k0[:, q, :]
        high_ref[q] = t1[:, TILE - W + q, :]
        high_ref[W + q] = k1[:, TILE - W + q, :]
    for q in range(W - 1):
        low_ref[2 * W + q] = s0[:, q, :]
        high_ref[2 * W + q] = s1[:, TILE - W + 1 + q, :]


def pack_lon_kernel(t0, k0, s0, t1, k1, s1, low_ref, high_ref):
    low_ref[0:W] = t0[...]
    low_ref[W:2 * W] = k0[...]
    low_ref[2 * W:] = s0[0:W - 1]
    high_ref[0:W] = t1[...]
    high_ref[W:2 * W] = k1[...]
    high_ref[2 * W:] = s1[1:W]


def pack(kernel, block, dim, t, k, s, slab, name):
    count = t.shape[dim] // block[dim]

    def spec(place):
        return pl.BlockSpec(block, lambda g: tuple(place if d == dim else 0 for d in range(3)))

    shape = jax.ShapeDtypeStruct((SENT,) + slab, jnp.float32)
    return pl.pallas_call(
        kernel,
        grid=(1,),
        out_shape=(shape, shape),
        in_specs=[spec(0)] * 3 + [spec(count - 1)] * 3,
        out_specs=[pl.BlockSpec(shape.shape, lambda g: (0, 0, 0))] * 2,
        name=name,
    )(t, k, s, t, k, s)


def face(p, q):
    summed = p + q
    return (2.0 * time_step) * p * q / jnp.where(summed > 0.0, summed, 1.0)


def conduct_kernel(n, m, lat, t_ref, k_ref, s_ref, below_ref, above_ref, south_ref, north_ref,
                   csouth_ref, cnorth_ref, v_ref, w_ref, out_ref, parts_ref,
                   ta, tb, k, s, hx, hy, hz, hd, full, z, sems):
    layers = t_ref.shape[2]
    planes = n + 2 * W
    end = TILE + m
    copies = [
        pltpu.make_async_copy(src, dst.at[W:n + W, TILE:end, :], sems.at[i])
        for i, (src, dst) in enumerate(((k_ref, k), (t_ref, ta), (s_ref, s)))
    ]
    for copy in copies:
        copy.start()
    for q in range(SENT):
        arr, at = ((ta, q), (k, q - W), (s, q - 2 * W))[q // W]
        late = q // W == 2
        low_row = PAD + at + (1 if late else 0)
        arr[W:n + W, low_row, :] = south_ref[q]
        arr[W:n + W, end + at, :] = north_ref[q]
        low_plane = at + (1 if late else 0)
        high_plane = n + W + at
        arr[low_plane, TILE:end, :] = below_ref[q]
        arr[high_plane, TILE:end, :] = above_ref[q]
        arr[low_plane, PAD:TILE, :] = csouth_ref[q, 0:W]
        arr[high_plane, PAD:TILE, :] = csouth_ref[q, W:2 * W]
        arr[low_plane, end:end + W, :] = cnorth_ref[q, 0:W]
        arr[high_plane, end:end + W, :] = cnorth_ref[q, W:2 * W]
    copies[0].wait()

    rows = slice(PAD, end + W)
    count = m + 2 * W
    inside = lax.broadcasted_iota(jnp.int32, (count, layers), 1) < layers - 1

    def faces(i, kc):
        kn = k[i + 1, rows, :]
        hx[i, rows, :] = face(kc, kn)
        hy[i, rows, :] = face(kc, k[i, PAD + 1:PAD + 1 + count, :])
        up = jnp.where(inside, face(kc, pltpu.roll(kc, layers - 1, 1)), 0.0)
        hz[i, rows, :] = up
        hd[i, rows, :] = pltpu.roll(up, 1, 1)
        return kn

    lax.fori_loop(0, planes - 1, faces, k[0, rows, :], unroll=8)

    copies[1].wait()
    copies[2].wait()
    for step in range(STEPS):
        last = step == STEPS - 1
        src, dst = (ta, tb) if step % 2 == 0 else (tb, ta)
        lo, num = (TILE, m) if last else (PAD, count)

        def body(p, carry):
            tc, before = carry
            tn = src[p + 1, lo:lo + num, :]
            fx = hx[p, lo:lo + num, :] * (tn - tc)
            fn = hy[p, lo:lo + num, :] * (src[p, lo + 1:lo + 1 + num, :] - tc)
            fs = hy[p, lo - 1:lo - 1 + num, :] * (src[p, lo - 1:lo - 1 + num, :] - tc)
            fu = hz[p, lo:lo + num, :] * (pltpu.roll(tc, layers - 1, 1) - tc)
            fd = hd[p, lo:lo + num, :] * (pltpu.roll(tc, 1, 1) - tc)
            gain = s[p, lo:lo + num, :]
            if step == 0:
                gain = gain * time_step
                s[p, lo:lo + num, :] = gain
            new = tc + ((gain + (fx - before)) + ((fn + fs) + (fu + fd)))
            if last:
                full[p - W] = new
            else:
                dst[p, lo:lo + num, :] = new
            return tn, fx

        tc = src[step + 1, lo:lo + num, :]
        start = hx[step, lo:lo + num, :] * (tc - src[step, lo:lo + num, :])
        lax.fori_loop(step + 1, planes - 1 - step, body, (tc, start), unroll=16)

    written = pltpu.make_async_copy(full, out_ref, sems.at[0])
    written.start()
    share = R // lat
    row = lax.broadcasted_iota(jnp.int32, (R, R), 0)
    col = lax.broadcasted_iota(jnp.int32, (R, R), 1)
    order = jnp.where(row % lat * share + row // lat == col, 1.0, 0.0).astype(jnp.float32)
    vh, vl = halves(dot(order, v_ref[...], 1, 0))
    lhs = jnp.concatenate([vh, vh, vl], axis=1)

    def project(i, c):
        pair = jnp.concatenate([full[2 * i], full[2 * i + 1]], axis=1)
        high, low = halves(pair)
        got = lax.dot_general(
            lhs, jnp.concatenate([high, low, high], axis=0), (((1,), (0,)), ((), ())),
            preferred_element_type=jnp.float32,
        )
        for e in range(2):
            for a in range(share):
                z[a, pl.ds(2 * i + e, lat, stride=n), :] = got[
                    a * lat:(a + 1) * lat, e * layers:(e + 1) * layers
                ]
        return c

    lax.fori_loop(0, n // 2, project, 0, unroll=8)
    tiled = jnp.concatenate([w_ref[...]] * share, axis=0)
    block = lax.broadcasted_iota(jnp.int32, tiled.shape, 0) // R
    total = None
    for a in range(share):
        part = dot3(z[a], jnp.where(block == a, tiled, 0.0), 1, 1)
        total = part if total is None else total + part
    parts_ref[...] = total
    written.wait()


def conduct(t, k, s, v, w):
    n, m, layers = t.shape
    lon, lat = lax.axis_size("lon"), lax.axis_size("lat")
    north_to = [(i, i + 1) for i in range(lat - 1)]
    south_to = [(j, i) for i, j in north_to]
    up = [(i, (i + 1) % lon) for i in range(lon)]
    down = [(j, i) for i, j in up]
    low, high = pack(pack_lat_kernel, (n, TILE, layers), 1, t, k, s, (n, layers), "pack_lat")
    south = lax.ppermute(high, "lat", north_to)
    north = lax.ppermute(low, "lat", south_to)
    low, high = pack(pack_lon_kernel, (W, m, layers), 0, t, k, s, (m, layers), "pack_lon")
    below = lax.ppermute(high, "lon", up)
    above = lax.ppermute(low, "lon", down)
    csouth = lax.ppermute(jnp.concatenate([below[:, m - W:], above[:, m - W:]], 1), "lat", north_to)
    cnorth = lax.ppermute(jnp.concatenate([below[:, :W], above[:, :W]], 1), "lat", south_to)
    share = R // lat
    big = pltpu.VMEM((n + 2 * W, m + 2 * TILE, layers), jnp.float32)
    vmem = pl.BlockSpec(memory_space=pltpu.VMEM)
    return pl.pallas_call(
        functools.partial(conduct_kernel, n, m, lat),
        out_shape=(
            jax.ShapeDtypeStruct(t.shape, jnp.float32),
            jax.ShapeDtypeStruct((lat * n, share * R), jnp.float32),
        ),
        in_specs=[pl.BlockSpec(memory_space=pl.ANY)] * 3 + [vmem] * 8,
        out_specs=[pl.BlockSpec(memory_space=pl.ANY), vmem],
        scratch_shapes=[big] * 8
        + [pltpu.VMEM(t.shape, jnp.float32), pltpu.VMEM((share, lat * n, layers), jnp.float32), pltpu.SemaphoreType.DMA((3,))],
        compiler_params=pltpu.CompilerParams(vmem_limit_bytes=56 * 2**20),
        name="conduct",
    )(t, k, s, below, above, south, north, csouth, cnorth, v.T, w.T)


def inverse_factor(gram):
    n = gram.shape[0]
    row = lax.broadcasted_iota(jnp.int32, (n, n), 0)
    inv = jnp.where(row == lax.broadcasted_iota(jnp.int32, (n, n), 1), 1.0, 0.0)
    scale = jnp.zeros((n, n), jnp.float32)
    columns = [jnp.broadcast_to(gram[:, k:k + 1], (n, n)) for k in range(n)]
    for j in range(n):
        top, at = j // 8 * 8, j % 8
        if at == 0 and j:
            columns = [c if c is None else c[8:] for c in columns]
        column = columns[j]
        pivot = column[at:at + 1]
        factor = jnp.where(row[top:] > j, column, 0.0) * (1.0 / pivot)
        for k in range(j + 1, n):
            columns[k] = columns[k] - factor * columns[k][at:at + 1]
        columns[j] = None
        scale = jnp.where(row == j, lax.rsqrt(pivot), scale)
        below = inv[top:] - factor * inv[j:j + 1]
        inv = below if top == 0 else jnp.concatenate([inv[:top], below], axis=0)
    return inv * scale


def call(kernel, name, outs, args, scratch=(), cost=None, aliases=None):
    vmem = pl.BlockSpec(memory_space=pltpu.VMEM)
    return pl.pallas_call(
        kernel,
        out_shape=tuple(jax.ShapeDtypeStruct(o, jnp.float32) for o in outs),
        in_specs=[vmem] * len(args),
        out_specs=(vmem,) * len(outs),
        scratch_shapes=list(scratch),
        compiler_params=pltpu.CompilerParams(vmem_limit_bytes=40 * 2**20),
        cost_estimate=cost,
        name=name,
    )(*args)


def cost(us):
    return pl.CostEstimate(flops=0, bytes_accessed=int(us * 3e6), transcendentals=0)


def add_up(ref):
    total = ref[0]
    for i in range(1, ref.shape[0]):
        total = total + ref[i]
    return total


def send_all(ref, x):
    for i in range(ref.shape[0]):
        ref[i] = x


def widen(x, n):
    k = x.shape[0] // n
    return jnp.concatenate([x[i * k:(i + 1) * k] for i in range(n)], axis=1)


def narrow(x, n):
    c = x.shape[1] // n
    return jnp.concatenate([x[:, i * c:(i + 1) * c] for i in range(n)], axis=0)


def eye(n):
    row = lax.broadcasted_iota(jnp.int32, (n, n), 0)
    return jnp.where(row == lax.broadcasted_iota(jnp.int32, (n, n), 1), 1.0, 0.0).astype(jnp.float32)


def flip(x):
    return dot(eye(x.shape[1]), x, 1, 1)


def diagonal(x, n):
    k = x.shape[0]
    wide = jnp.concatenate([x] * n, axis=1)
    wide = jnp.concatenate([wide] * n, axis=0)
    row = lax.broadcasted_iota(jnp.int32, wide.shape, 0) // k
    col = lax.broadcasted_iota(jnp.int32, wide.shape, 1) // k
    return jnp.where(row == col, wide, 0.0)


def stack_left(x):
    high, low = halves(x)
    return jnp.concatenate([high, high, low], axis=1)


def stack_right(x):
    high, low = halves(x)
    return jnp.concatenate([high, low, high], axis=0)


def product(left, right):
    return lax.dot_general(
        left, right, (((1,), (0,)), ((), ())), preferred_element_type=jnp.float32
    )


def lon_project_kernel(got, ut, y1, out):
    y = add_up(got)
    y1[...] = y
    send_all(out, dot(ut[...], y, 1, 0))


def lon_block_kernel(got, y1, out):
    send_all(out, widen(dot(add_up(got), y1[...], 1, 1), 2))


def radial_kernel(m, t, wt, out):
    n = t.shape[0] // m
    half = m // 2
    share = out.shape[0]
    peers = R // share
    w = halves(wt[...])

    def body(j, c):
        x = jnp.concatenate(
            [t[pl.ds(j + h * half, n, stride=m), :] for h in range(2)], axis=0
        )
        got = dot3(w, x, 1, 1)
        for b in range(share):
            out[b, pl.ds(j, peers, stride=half), :] = got[b * peers:(b + 1) * peers]
        return c

    lax.fori_loop(0, half, body, 0, unroll=4)


def lat_modes_kernel(got, rt, out, b1):
    block = narrow(add_up(got), 2)
    b1[...] = block
    gram = widen(dot(block, block, 1, 1), 4)
    wide = jnp.concatenate([block, block], axis=1)
    wide = jnp.concatenate([wide] * 4, axis=0)
    row = lax.broadcasted_iota(jnp.int32, wide.shape, 0) // R
    half = lax.broadcasted_iota(jnp.int32, wide.shape, 1) // block.shape[1]
    total = None
    for b in range(rt.shape[0]):
        part = dot3(rt[b], jnp.where(row == 2 * b + half, wide, 0.0), 1, 1)
        total = part if total is None else total + part
    rows = total.shape[0] // out.shape[0]
    for i in range(out.shape[0]):
        out[i, 0:rows] = total[i * rows:(i + 1) * rows]
        out[i, rows:] = gram


def lat_project_kernel(got, b1, vt, out, y2, lon, lont):
    total = add_up(got)
    gram = narrow(total[total.shape[0] - R // 4:], 4)
    inv = inverse_factor(gram)
    block = b1[...]
    lont[...] = dot(inv, block, 1, 0)
    lon[...] = dot(flip(block), inv, 1, 1)
    y = dot(total[:total.shape[0] - R // 4], diagonal(inv, 4), 1, 1)
    y2[...] = y
    half = vt.shape[1] // 2
    lane = lax.broadcasted_iota(jnp.int32, (R, y.shape[1]), 1) // R % 2
    send_all(
        out,
        jnp.where(
            lane == 0, dot(vt[:, 0:half], y, 1, 0), dot(vt[:, half:], y, 1, 0)
        ),
    )


def lon_sums_kernel(m, t, lont, out):
    n = t.shape[0] // m
    layers = t.shape[1]
    left = stack_left(lont[...])

    def body(j, c):
        x = jnp.concatenate([t[pl.ds(2 * j + e, n, stride=m), :] for e in range(2)], axis=1)
        got = product(left, stack_right(x))
        for e in range(2):
            out[pl.ds(2 * j + e, R, stride=m), :] = got[:, e * layers:(e + 1) * layers]
        return c

    lax.fori_loop(0, m // 2, body, 0, unroll=4)


def lat_block_kernel(got, y2, out):
    q = add_up(got)
    y = y2[...]
    lane = lax.broadcasted_iota(jnp.int32, q.shape, 1) // R % 2
    width = q.shape[1]
    both = q + jnp.where(lane == 0, pltpu.roll(q, width - R, 1), pltpu.roll(q, R, 1))
    side = lax.broadcasted_iota(jnp.int32, y.shape, 1) // R % 2
    rows = jnp.concatenate([jnp.where(side == 0, y, 0.0), jnp.where(side == 1, y, 0.0)], axis=0)
    send_all(out, widen(dot(both, rows, 1, 1), 2))


def radial_modes_kernel(got, lp, out, b2, g2):
    block = narrow(add_up(got), 2)
    b2[...] = block
    g2[...] = widen(dot(block, block, 1, 1), 4)
    left = stack_left(block)
    m = block.shape[1]
    layers = lp.shape[1]

    def body(a, c):
        x = jnp.concatenate(
            [lp[pl.ds(pl.multiple_of((2 * a + e) * m, m), m), :] for e in range(2)], axis=1
        )
        y = product(left, stack_right(x))
        for e in range(2):
            out[a, e * R:(e + 1) * R, :] = y[:, e * layers:(e + 1) * layers]
        return c

    lax.fori_loop(0, R // 2, body, 0, unroll=16)


def radial_sum_kernel(got, out):
    send_all(out, add_up(got))


def lat_factor_kernel(g2, b2, inv, lat):
    inverse = inverse_factor(narrow(g2[...], 4))
    inv[...] = inverse
    lat[...] = dot(flip(b2[...]), inverse, 1, 1)


def last_kernel(m, y3_ref, inv2, lat, lon, wt, t, err, rad, core_ref, y3, first, second):
    layers = y3.shape[1]
    n = t.shape[0] // m
    mix = halves(diagonal(inv2[...], layers // R))
    for i in range(y3.shape[0] // layers):
        y3[i * layers:(i + 1) * layers] = dot3(mix, y3_ref[i * layers:(i + 1) * layers])
    y = halves(y3[...])
    proj = dot3(wt[...], y, 1, 1)
    block = dot3(proj, y)
    inv = inverse_factor(dot(block, block, 1, 1))
    radt = dot(inv, block, 1, 0)
    rad[...] = radt
    radh = halves(radt)
    core = dot3(y, radh, 1, 1)
    core_ref[...] = core
    first[...] = dot3(core, radh)
    left = stack_left(lat[...])

    def widen_lat(a, c):
        x = jnp.concatenate(
            [first[pl.ds(pl.multiple_of((2 * a + e) * R, R), R), :] for e in range(2)], axis=1
        )
        got = product(left, stack_right(x))
        for e in range(2):
            at = pl.multiple_of((2 * a + e) * m, m)
            second[pl.ds(at, m), :] = got[:, e * layers:(e + 1) * layers]
        return c

    lax.fori_loop(0, R // 2, widen_lat, 0, unroll=16)
    lonl = stack_left(lon[...])

    def widen_lon(j, c):
        x = jnp.concatenate(
            [second[pl.ds(2 * j + e, R, stride=m), :] for e in range(2)], axis=1
        )
        got = product(lonl, stack_right(x))
        for e in range(2):
            at = pl.ds(2 * j + e, n, stride=m)
            err[at, :] = t[at, :] - got[:, e * layers:(e + 1) * layers]
        return c

    lax.fori_loop(0, m // 2, widen_lon, 0, unroll=16)


def exchange(parts, axis):
    return lax.all_to_all(parts, axis, 0, 0, tiled=True)


def local(t0, k, s, u, v, w):
    n, m, layers = t0.shape
    lon, lat = lax.axis_size("lon"), lax.axis_size("lat")
    t, parts = conduct(t0, k, s, v, w)
    flat = t.reshape(n * m, layers)
    share = R // lon
    wt = w.T
    vt = v.T
    wide = R // lat * R
    got = exchange(parts.reshape(lat, n, wide), "lat")
    (rt,) = call(
        functools.partial(radial_kernel, m), "radial",
        [(share, lon * m // 2, 2 * n)],
        [flat, wt.reshape(lon, share, layers).transpose(1, 0, 2).reshape(R, layers)],
        cost=cost(4),
    )
    y1, parts = call(
        lon_project_kernel, "lon_project", [(n, wide), (lon, R, wide)], [got, u.T]
    )
    (parts,) = call(
        lon_block_kernel, "lon_block", [(lat, R // 2, 2 * n)], [exchange(parts, "lon"), y1]
    )
    parts, b1 = call(
        lat_modes_kernel, "lat_modes", [(lon, m // 2 + R // 4, 2 * share * R), (R, n)],
        [exchange(parts, "lat"), rt],
    )
    parts, y2, new_lon, lont = call(
        lat_project_kernel, "lat_project",
        [(lat, R, 2 * share * R), (m // 2, 2 * share * R), (n, R), (R, n)],
        [exchange(parts, "lon"), b1, vt],
    )
    got = exchange(parts, "lat")
    (lp,) = call(
        functools.partial(lon_sums_kernel, m), "lon_sums", [(R * m, layers)], [flat, lont],
        cost=cost(4),
    )
    (parts,) = call(lat_block_kernel, "lat_block", [(lon, R // 2, 2 * m)], [got, y2])
    parts, b2, g2 = call(
        radial_modes_kernel, "radial_modes",
        [(lon, share * R, layers), (R, m), (R // 4, 4 * R)],
        [exchange(parts, "lon"), lp],
    )
    both = ("lon", "lat")
    got = exchange(parts.reshape(lon * lat, share * R // lat, layers), both)
    hop = 1
    while hop < lat:
        g2 = g2 + lax.ppermute(g2, "lat", [(i, i ^ hop) for i in range(lat)])
        hop *= 2
        if 2 * hop == lat:
            g2, got = lax.optimization_barrier((g2, got))
    (parts,) = call(radial_sum_kernel, "radial_sum", [got.shape], [got])
    got = exchange(parts, both)
    inv2, new_lat = call(
        lat_factor_kernel, "lat_factor", [(R, R), (m, R)], [g2, b2], cost=cost(4)
    )
    err, new_rad, core = call(
        functools.partial(last_kernel, m), "last",
        [(n * m, layers), (R, layers), (R * R, R)],
        [got.reshape(R * R, layers), inv2, new_lat, new_lon, wt, flat],
        scratch=[
            pltpu.VMEM((R * R, layers), jnp.float32),
            pltpu.VMEM((R * R, layers), jnp.float32),
            pltpu.VMEM((R * m, layers), jnp.float32),
        ],
    )
    return (t, err.reshape(n, m, layers), new_lon, new_lat, new_rad.T, core.reshape(R, R, R))


def solution(mesh):
    grid = P("lon", "lat", None)
    return jax.shard_map(
        local,
        mesh=mesh,
        in_specs=(grid, grid, grid, P("lon", None), P("lat", None), P()),
        out_specs=(grid, grid, P("lon", None), P("lat", None), P(), P()),
        check_vma=False,
    )
```
